256 devices in a mesh: row: 16 (over z, core), rep: 16 (over x, y).
Axes of the slice: x: 4, y: 4, z: 8, core: 2. Of those that a mesh axis runs over, the one named last changes fastest.
Arguments:
- tile_values: bfloat16 [16, 16, 20, 512, 512], P('row', 'rep'), may hold values from -0.125 to 0.125
- tile_rows: int32 [16, 16, 20], P('row', 'rep'), may hold values from 0 to 15, as said below
- tile_cols: int32 [16, 16, 20], P('row', 'rep'), may hold values from 0 to 15
- tile_counts: int32 [16, 16], P('row', 'rep'), may hold values from 1 to 20, as said below
- features: bfloat16 [131072, 256], P(('row', 'rep')), may hold values from -6 to 6
- weight: bfloat16 [256, 256], replicated, may hold values from -0.375 to 0.375
- cotangent: bfloat16 [131072, 256], P(('row', 'rep')), may hold values from -6 to 6
Outputs:
- output: bfloat16 [131072, 256], P(('row', 'rep'))
- grad_features: bfloat16 [131072, 256], P(('row', 'rep'))
- grad_weight: float32 [256, 256], replicated
The draws below stay inside these ranges and needn't reach their ends.
Inputs may be any that keep to these rules, and one draw needn't show every extreme that they name: `tile_rows`: within one device the first tile_counts slots name distinct tiles; slots past the count are not part of A. `tile_counts`: some device uses all 20 slots.
All inputs are finite; a program needn't handle non-finite values.
Results may differ from the reference program's by a relative error of at most 0.025.
Values may be sent and summed in bfloat16 or wider, within the bound.
No kernel may reach another device: no remote copies, remote signals or barrier semaphores. Data moves between devices by JAX's collectives and lax.ppermute only.
A program may use at most 64 MiB of HBM per device.

```python
import math
import jax
import jax.numpy as jnp
from jax import lax

F = 256
TILE = 512
TMAX = 20
GROUPS = 16
REPLICAS = 16
NODES = 131072


def tile_slots(key):
    total = GROUPS * REPLICAS
    keys = jax.random.split(key, total)
    picked = jax.vmap(lambda k: jax.random.permutation(k, total)[:TMAX])(keys)
    return picked.reshape(GROUPS, REPLICAS, TMAX).astype(jnp.int32)


def draw_tile_rows(key, part):
    slots = tile_slots(key)
    return (slots // GROUPS).astype(jnp.int32)


def draw_tile_cols(key, part):
    slots = tile_slots(key)
    return (slots % GROUPS).astype(jnp.int32)


def draw_tile_counts(key, part):
    key = jax.random.fold_in(key, 11)
    first, second, third, fourth = jax.random.split(key, 4)
    total = GROUPS * REPLICAS
    lowest = TMAX // 5 + 1
    base = jax.random.randint(first, (total,), lowest, lowest + TMAX // 3 + 1)
    heavy = jax.random.randint(second, (total,), TMAX // 2, TMAX + 1)
    picks = jax.random.randint(third, (total,), 0, 8) == 0
    counts = jnp.where(picks, heavy, base)
    busiest = jax.random.randint(fourth, (), 0, total)
    counts = jnp.where(jnp.arange(total) == busiest, TMAX, counts)
    return counts.reshape(GROUPS, REPLICAS).astype(jnp.int32)


def shard_levels(rng, extent, cuts, least, largest):
    loudness = 1.0
    for position, parts in cuts:
        heights = jax.random.uniform(jax.random.fold_in(jax.random.fold_in(rng, 6), position), (parts,), jnp.float32, least / len(cuts), largest / len(cuts))
        loudness = loudness * jnp.repeat(jnp.exp(heights), extent[position] // parts).reshape((-1,) + (1,) * (len(extent) - 1 - position))
    return loudness


def normal_values(stream_key, shape, width, reach, cuts=(), held_as=jnp.bfloat16):
    array = jax.random.normal(stream_key, shape, jnp.float32) * width
    if len(cuts) > 0:
        array = shard_levels(stream_key, shape, cuts, -0.22, 0.18) * array
    return jnp.clip(array, min=-reach, max=reach).astype(held_as)


def setup_inputs(seed: int = 0) -> dict:
    seeds = jax.random.split(jax.random.key(seed), 8)
    tile_values = normal_values(seeds[0], (GROUPS, REPLICAS, TMAX, TILE, TILE), (4 * TILE) ** -0.5, 0.125, ((0, 16), (1, 16)))
    tile_rows = draw_tile_rows(jax.random.fold_in(seeds[7], 71), 0)
    tile_cols = draw_tile_cols(jax.random.fold_in(seeds[7], 71), 0)
    tile_counts = draw_tile_counts(jax.random.fold_in(seeds[7], 71), 0)
    features = normal_values(seeds[4], (NODES, F), 1.0, 6.0, ((0, 256),))
    weight = normal_values(seeds[5], (F, F), F ** -0.5, 0.375)
    cotangent = normal_values(seeds[6], (NODES, F), 1.0, 6.0, ((0, 256),))
    return dict(tile_values=tile_values, tile_rows=tile_rows, tile_cols=tile_cols, tile_counts=tile_counts, features=features, weight=weight, cotangent=cotangent)


def device_partial(source, tiles, dest_tile, src_start, count, span, transpose):

    def step(carry, item):
        tile, dest, src, slot = item

        def add(acc):
            piece = lax.dynamic_slice_in_dim(source, src, TILE, 0)
            if transpose:
                prod = jnp.dot(tile.T, piece, preferred_element_type=jnp.float32)
            else:
                prod = jnp.dot(tile, piece, preferred_element_type=jnp.float32)
            current = lax.dynamic_slice_in_dim(acc, dest, TILE, 0)
            return lax.dynamic_update_slice_in_dim(acc, current + prod, dest, 0)
        return (lax.cond(slot < count, add, lambda acc: acc, carry), None)
    slots = jnp.arange(TMAX, dtype=jnp.int32)
    start = jnp.zeros((span, F), jnp.float32)
    partial_sum, _ = lax.scan(step, start, (tiles, dest_tile, src_start, slots))
    return partial_sum.astype(jnp.bfloat16).astype(jnp.float32)

def reference(tile_values, tile_rows, tile_cols, tile_counts, features, weight, cotangent):
    total = GROUPS * REPLICAS
    flat_values = tile_values.reshape(total, TMAX, TILE, TILE)
    flat_rows = tile_rows.reshape(total, TMAX).astype(jnp.int32)
    flat_cols = tile_cols.reshape(total, TMAX).astype(jnp.int32)
    flat_counts = tile_counts.reshape(total).astype(jnp.int32)
    device_ids = jnp.arange(total, dtype=jnp.int32)

    def forward_step(result, item):
        tiles, rows, cols, count, dev = item
        group = dev // REPLICAS
        rep = dev % REPLICAS
        src = ((cols * REPLICAS + rep) * TILE).astype(jnp.int32)
        part = device_partial(features, tiles, (rows * TILE).astype(jnp.int32), src, count, REPLICAS * TILE, False)
        lower = (group * REPLICAS * TILE).astype(jnp.int32)
        current = lax.dynamic_slice_in_dim(result, lower, REPLICAS * TILE, 0)
        return (lax.dynamic_update_slice_in_dim(result, current + part, lower, 0), None)
    summed, _ = lax.scan(forward_step, jnp.zeros((NODES, F), jnp.float32), (flat_values, flat_rows, flat_cols, flat_counts, device_ids))
    agg = (summed + features.astype(jnp.float32)).astype(jnp.bfloat16)
    pre = jnp.dot(agg, weight, preferred_element_type=jnp.float32)
    sig = jax.nn.sigmoid(pre)
    output = (pre * sig).astype(jnp.bfloat16)
    slope = (cotangent.astype(jnp.float32) * sig * (1.0 + pre * (1.0 - sig))).astype(jnp.bfloat16)
    grad_weight = jnp.dot(agg.T, slope, preferred_element_type=jnp.float32) / math.sqrt(NODES)
    adjoint = jnp.dot(slope, weight.T, preferred_element_type=jnp.float32).astype(jnp.bfloat16)

    def backward_step(result, item):
        tiles, rows, cols, count, dev = item
        group = dev // REPLICAS
        rep = dev % REPLICAS
        src = ((group * REPLICAS + rows) * TILE).astype(jnp.int32)
        part = device_partial(adjoint, tiles, (cols * TILE).astype(jnp.int32), src, count, GROUPS * TILE, True)
        part = part.reshape(GROUPS, 1, TILE, F)
        current = lax.dynamic_slice_in_dim(result, rep, 1, 1)
        return (lax.dynamic_update_slice_in_dim(result, current + part, rep, 1), None)
    back, _ = lax.scan(backward_step, jnp.zeros((GROUPS, REPLICAS, TILE, F), jnp.float32), (flat_values, flat_rows, flat_cols, flat_counts, device_ids))
    back = back.reshape(NODES, F)
    grad_features = (adjoint.astype(jnp.float32) + back).astype(jnp.bfloat16)
    return (output, grad_features, grad_weight)
```

```python
import math

import jax
import jax.numpy as jnp
from jax import lax
from jax.experimental import pallas as pl
from jax.experimental.pallas import tpu as pltpu
from jax.sharding import Mesh
from jax.sharding import PartitionSpec as P

AXES = ("z", "c", "x", "y")
SIZES = (8, 2, 4, 4)
BF = jnp.bfloat16
F32 = jnp.float32
VMEM_LIMIT = 44 * 1024 * 1024


def rank(q):
    out = 0
    for v, s in zip(q, SIZES):
        out = out * s + v
    return out


def pairs(move):
    z, c, x, y = SIZES
    every = [(i, j, k, l) for i in range(z) for j in range(c) for k in range(x) for l in range(y)]
    return [(rank(q), rank(move(q))) for q in every]


def z_move():
    return pairs(lambda q: ((q[0] + 1 - 2 * q[1]) % 8, q[1], q[2], q[3]))


def core_move():
    return pairs(lambda q: (q[0], 1 - q[1], q[2], q[3]))


def plane_move(stage, d):
    def move(q):
        z, c, x, y = q
        if (c == 0) == (stage == 0):
            return (z, c, (x + d) % 4, y)
        return (z, c, x, (y + d) % 4)

    return pairs(move)


def send(v, perm):
    return lax.ppermute(v, AXES, perm)


def cat(*parts):
    return jnp.concatenate(parts, axis=0)


def add(*parts):
    total = parts[0].astype(F32)
    for p in parts[1:]:
        total = total + p.astype(F32)
    return total


def tile_kernel(copies, cuts, n_parts, block, transpose, info, *refs):
    parts, tiles, outs = refs[:n_parts], refs[n_parts], refs[n_parts + 1 : n_parts + 1 + len(cuts)]
    panel, acc, held, part_sem, tile_sem = refs[n_parts + 1 + len(cuts) :]
    slots = held.shape[0]
    count = info[2 * slots]

    def tile_copy(k):
        return pltpu.make_async_copy(tiles.at[k], held.at[k], tile_sem.at[k])

    def begin(k, carry):
        tile_copy(k).start()
        return carry

    started = []
    for i, (part, src, size, dst) in enumerate(copies):
        copy = pltpu.make_async_copy(
            parts[part].at[pl.ds(src, size)], panel.at[pl.ds(dst, size)], part_sem.at[i]
        )
        copy.start()
        started.append(copy)
    lax.fori_loop(0, count, begin, 0)
    acc[...] = jnp.zeros_like(acc)
    for copy in started:
        copy.wait()

    def step(k, carry):
        tile_copy(k).wait()
        src = pl.multiple_of(info[k] * block, block)
        dst = pl.multiple_of(info[slots + k] * block, block)
        piece = panel[pl.ds(src, block), :]
        dims = (((0,), (0,)), ((), ())) if transpose else (((1,), (0,)), ((), ()))
        acc[pl.ds(dst, block), :] += lax.dot_general(
            held[k], piece, dims, preferred_element_type=F32
        )
        return carry

    lax.fori_loop(0, count, step, 0)
    for out, (start, rows) in zip(outs, cuts):
        out[...] = acc[pl.ds(start, rows), :].astype(BF)


def tile_terms(info, parts, copies, tiles, cuts, transpose):
    slots, block = tiles.shape[0], tiles.shape[1]
    rows = sum(c[2] for c in copies)
    width = parts[0].shape[1]

    def kernel(*refs):
        tile_kernel(copies, cuts, len(parts), block, transpose, *refs)

    return pl.pallas_call(
        kernel,
        out_shape=[jax.ShapeDtypeStruct((n, width), BF) for _, n in cuts],
        in_specs=[pl.BlockSpec(memory_space=pltpu.SMEM)]
        + [pl.BlockSpec(memory_space=pl.ANY)] * (len(parts) + 1),
        out_specs=[pl.BlockSpec(memory_space=pltpu.VMEM)] * len(cuts),
        scratch_shapes=[
            pltpu.VMEM((rows, width), BF),
            pltpu.VMEM((rows, width), F32),
            pltpu.VMEM((slots, block, block), BF),
            pltpu.SemaphoreType.DMA((len(copies),)),
            pltpu.SemaphoreType.DMA((slots,)),
        ],
        compiler_params=pltpu.CompilerParams(vmem_limit_bytes=VMEM_LIMIT),
        cost_estimate=pl.CostEstimate(
            flops=2 * slots * block * block * width,
            bytes_accessed=2 * slots * block * block + 4 * rows * width,
            transcendentals=0,
        ),
        name="tiles_t" if transpose else "tiles",
    )(info, *parts, tiles)


def node_kernel(s0, s1, s2, s3, features, weight, cotangent, output, message):
    rows = features.shape[0]
    half = rows // 2
    term = jnp.zeros(weight.shape, F32)
    for i in range(2):
        at = pl.ds(i * half, half)
        summed = add(s0[at, :], s1[at, :]) + add(s2[at, :], s3[at, :])
        agg = (summed + features[at, :].astype(F32)).astype(BF)
        pre = jnp.dot(agg, weight[...], preferred_element_type=F32)
        sig = jax.nn.sigmoid(pre)
        output[at, :] = (pre * sig).astype(BF)
        slope = (cotangent[at, :].astype(F32) * sig * (1.0 + pre * (1.0 - sig))).astype(BF)
        message[at, :] = lax.dot_general(
            slope, weight[...], (((1,), (1,)), ((), ())), preferred_element_type=F32
        ).astype(BF)
        term = term + lax.dot_general(
            agg, slope, (((0,), (0,)), ((), ())), preferred_element_type=F32
        )
    message[pl.ds(rows, weight.shape[0]), :] = term.astype(BF)


def node_step(sums, features, weight, cotangent):
    rows, width = features.shape
    return pl.pallas_call(
        node_kernel,
        out_shape=[
            jax.ShapeDtypeStruct((rows, width), BF),
            jax.ShapeDtypeStruct((rows + weight.shape[0], width), BF),
        ],
        compiler_params=pltpu.CompilerParams(vmem_limit_bytes=16 * 1024 * 1024),
        cost_estimate=pl.CostEstimate(
            flops=6 * rows * width * width, bytes_accessed=20 * rows * width, transcendentals=rows * width
        ),
        name="nodes",
    )(*sums, features, weight, cotangent)


def row_place(cols, z, c, sign):
    d = ((cols // 2 - z) * sign) % 8
    other = jnp.where(cols % 2 == c, 0, 1)
    near = 2 * d + other
    near = jnp.where(d == 4, 15 - other, near)
    return jnp.where(d > 4, 8 + 2 * (7 - d) + 1 - other, near)


def gather_row(block):
    n = block.shape[0]
    half = n // 2
    other = send(block, core_move())
    parts, copies = [block, other], [(0, 0, n, 0), (1, 0, n, n)]

    def place(part, index, h):
        at = h * half
        if index == 4:
            copies.append((len(parts), 0, half, 15 * n + at))
        elif index == -4:
            copies.append((len(parts), 0, half, 14 * n + at))
        else:
            first = 2 * index if index > 0 else 8 + 2 * (-index - 1)
            copies.append((len(parts), 0, half, first * n + at))
            copies.append((len(parts), half, half, (first + 1) * n + at))
        parts.append(part)

    held = [cat(block[h * half : (h + 1) * half], other[h * half : (h + 1) * half]) for h in (0, 1)]
    for k in (1, 2, 3, 4):
        for h in (0, 1):
            held[h] = send(held[h] if k < 4 else held[h][:half], z_move())
            place(held[h], k, h)
            place(send(held[h], core_move()), -k, h)
    return parts, copies


def scatter_row(own, far, near, far_own, term, weight_term):
    n = far_own.shape[0]
    half = n // 2
    wh = weight_term.shape[0] // 2
    got = send(far, core_move())
    total = []
    ws = [[], []]
    for h in (0, 1):
        at = h * half

        def mine(k, o, at=at):
            i = ((k - 1) * 2 + o) * n + at
            return add(near[i : i + half], got[i : i + half])

        w = weight_term[h * wh : (h + 1) * wh]
        start = add(far_own[at : at + half], got[6 * n + at : 6 * n + at + half])
        held = send(cat(start.astype(BF), w), z_move())
        ws[h].append(held[half:])
        first = cat((mine(3, 0) + add(held[:half])).astype(BF), mine(3, 1).astype(BF), held[half:])
        held = send(first, z_move())
        ws[h].append(held[n:])
        for k in (2, 1):
            step = (cat(mine(k, 0), mine(k, 1)) + add(held[:n])).astype(BF)
            held = send(cat(step, held[n:]), z_move())
            ws[h].append(held[n:])
        total.append(held)
    back = cat(*[add(own[n + h * half : n + (h + 1) * half], total[h][half:n]).astype(BF) for h in (0, 1)])
    back = send(back, core_move())
    out = cat(*[add(own[h * half : (h + 1) * half], total[h][:half]) for h in (0, 1)])
    out = out + (add(term) + add(back))
    near_w = cat(*[ws[h][k] for h in (0, 1) for k in (0, 1, 2)])
    far_w = send(near_w, core_move())
    halves = []
    for h in (0, 1):
        w0 = weight_term[h * wh : (h + 1) * wh]
        m = ws[h][:3]
        s = [far_w[(h * 3 + k) * wh : (h * 3 + k + 1) * wh] for k in range(3)]
        even = add(w0, ws[h][3]) + add(m[1], s[1])
        odd = add(s[0], m[2]) + add(s[2], m[0])
        halves.append(even + odd)
    return out, cat(*halves)


def scatter_plane(outs):
    x0, y0, x1, y1, x3, y3, x2u, x2d, y2u, y2d = outs
    n = x2u.shape[0]
    up, down = plane_move(0, 1), plane_move(0, -1)

    def ring(q0, q1, q3, far_up, far_down):
        p = send(far_up, up)
        m = send(far_down, down)
        p = send(cat(add(q1[:n], p).astype(BF), q1[n:]), up)
        m = send(cat(q3[:n], add(q3[n:], m).astype(BF)), down)
        return [add(q0[i : i + n], p[i : i + n], m[i : i + n]).astype(BF) for i in (0, n)]

    s1, s2 = ring(x0, x1, x3, x2u, x2d)
    s3, s0 = ring(y0, y1, y3, y2u, y2d)
    return [
        s0,
        send(s1, plane_move(1, 1)),
        send(s2, plane_move(1, 2)),
        send(s3, plane_move(1, -1)),
    ]


def gather_plane(message, n):
    copies = []
    right = send(message, plane_move(1, -1))
    left = send(message, plane_move(1, 1))
    far = send(message, plane_move(1, 2))
    w = (add(message[n:], far[n:]) + add(right[n:], left[n:])).astype(BF)
    parts = [message, right, far, left]
    copies = [(db, 0, n, db * n) for db in range(4)]

    def lay(part, da, db, src=0, size=n, to=0):
        copies.append((part, src, size, (da * 4 + db) * n + to))

    up, down = plane_move(0, 1), plane_move(0, -1)
    first = cat(message[:n], right[:n])
    f_r, f_l = send(first, up), send(first, down)
    f_u, f_d = send(f_r[:n], up), send(f_l[n:], down)
    base = len(parts)
    parts += [f_l, f_r, f_u, f_d]
    lay(base, 1, 0)
    lay(base, 1, 1, n)
    lay(base + 1, 3, 0)
    lay(base + 1, 3, 1, n)
    lay(base + 2, 2, 0)
    lay(base + 3, 2, 1)
    second = cat(far[:n], left[:n], w)
    half = second.shape[0] // 2
    s_r, s_l = send(second, up), send(second, down)
    s_u, s_d = send(s_r[:half], up), send(s_l[half:], down)
    base = len(parts)
    parts += [s_l, s_r, s_u, s_d]
    lay(base, 1, 2)
    lay(base, 1, 3, n)
    lay(base + 1, 3, 2)
    lay(base + 1, 3, 3, n)
    lay(base + 2, 2, 2)
    lay(base + 2, 2, 3, n, half - n)
    lay(base + 3, 2, 3, 0, 2 * n - half, half - n)
    w = (add(w, s_d[2 * n - half :]) + add(s_l[2 * n :], s_r[2 * n :])).astype(BF)
    return parts, copies, w


def local(tile_values, tile_rows, tile_cols, tile_counts, features, weight, cotangent):
    tiles = tile_values[0, 0]
    rows, cols, count = tile_rows[0, 0], tile_cols[0, 0], tile_counts[0]
    n, width = features.shape
    scale = 1.0 / math.sqrt(n * 256)
    z, c, x, y = (lax.axis_index(a) for a in AXES)
    sign = 1 - 2 * c
    dx, dy = (rows // 4 - x) % 4, (rows % 4 - y) % 4
    da, db = jnp.where(c == 0, dx, dy), jnp.where(c == 0, dy, dx)
    fwd = jnp.concatenate([row_place(cols, z, c, -sign), da * 4 + (db + 3) % 4, count])
    bwd = jnp.concatenate([da * 4 + db, row_place(cols, z, c, sign), count])

    parts, copies = gather_row(features)
    fwd_cuts = [
        (0, 2 * n), (2 * n, 2 * n),
        (4 * n, 2 * n), (6 * n, 2 * n),
        (12 * n, 2 * n), (14 * n, 2 * n),
        (8 * n, n), (9 * n, n), (10 * n, n), (11 * n, n),
    ]
    sums = scatter_plane(tile_terms(fwd, parts, copies, tiles, fwd_cuts, False))
    output, message = node_step(sums, features, weight, cotangent)
    parts, copies, w = gather_plane(message, n)
    w = add(w, send(w, core_move())).astype(BF)
    bwd_cuts = [(0, 2 * n), (8 * n, 7 * n), (2 * n, 6 * n), (15 * n, n)]
    own, far, near, far_own = tile_terms(bwd, parts, copies, tiles, bwd_cuts, True)
    grad, w = scatter_row(own, far, near, far_own, message[:n], w)
    return (output, grad.astype(BF), w * scale)


def solution(mesh):
    grid = Mesh(mesh.devices.reshape(SIZES), AXES)
    row, rep = ("z", "c"), ("x", "y")
    placed = (
        P(row, rep, None, None, None),
        P(row, rep, None),
        P(row, rep, None),
        P(row, rep),
        P(AXES, None),
        P(),
        P(AXES, None),
    )
    return jax.shard_map(
        local,
        mesh=grid,
        in_specs=placed,
        out_specs=(P(AXES, None), P(AXES, None), P()),
        check_vma=False,
    )
```

```python
import math

import jax
import jax.numpy as jnp
from jax import lax
from jax.experimental import pallas as pl
from jax.experimental.pallas import tpu as pltpu
from jax.sharding import Mesh
from jax.sharding import PartitionSpec as P

AXES = ("z", "c", "x", "y")
SIZES = (8, 2, 4, 4)
BF = jnp.bfloat16
F32 = jnp.float32
VMEM_LIMIT = 44 * 1024 * 1024


def rank(q):
    out = 0
    for v, s in zip(q, SIZES):
        out = out * s + v
    return out


def pairs(move):
    z, c, x, y = SIZES
    every = [(i, j, k, l) for i in range(z) for j in range(c) for k in range(x) for l in range(y)]
    return [(rank(q), rank(move(q))) for q in every]


def z_move():
    return pairs(lambda q: ((q[0] + 1 - 2 * q[1]) % 8, q[1], q[2], q[3]))


def core_move():
    return pairs(lambda q: (q[0], 1 - q[1], q[2], q[3]))


def plane_move(stage, d):
    def move(q):
        z, c, x, y = q
        if (c == 0) == (stage == 0):
            return (z, c, (x + d) % 4, y)
        return (z, c, x, (y + d) % 4)

    return pairs(move)


def send(v, perm):
    return lax.ppermute(v, AXES, perm)


def cat(*parts):
    return jnp.concatenate(parts, axis=0)


def add(*parts):
    total = parts[0].astype(F32)
    for p in parts[1:]:
        total = total + p.astype(F32)
    return total


def join(segments, *arrays, after=()):
    width = arrays[0].shape[1]

    def total(refs, terms, rows):
        picked = []
        for i, at in terms:
            if isinstance(i, tuple):
                picked.append(total(refs, (i, at), rows))
            else:
                picked.append(refs[i][at : at + rows, :])
        return picked[0] if len(picked) == 1 else add(*picked)

    def kernel(*refs):
        out = refs[-1]
        base = 0
        for rows, terms in segments:
            out[base : base + rows, :] = total(refs, terms, rows).astype(BF)
            base += rows

    rows = sum(r for r, _ in segments)
    return pl.pallas_call(
        kernel,
        out_shape=jax.ShapeDtypeStruct((rows, width), BF),
        in_specs=[pl.BlockSpec(memory_space=pltpu.VMEM)] * len(arrays)
        + [pl.BlockSpec(memory_space=pl.ANY)] * len(after),
        out_specs=pl.BlockSpec(memory_space=pltpu.VMEM),
        compiler_params=pltpu.CompilerParams(vmem_limit_bytes=16 * 1024 * 1024),
        cost_estimate=pl.CostEstimate(
            flops=2 * rows * width, bytes_accessed=6 * rows * width, transcendentals=0
        ),
        name="join",
    )(*arrays, *after)


def tile_kernel(copies, cuts, n_parts, block, transpose, info, *refs):
    parts, tiles, outs = refs[:n_parts], refs[n_parts], refs[n_parts + 1 : n_parts + 1 + len(cuts)]
    panel, acc, held, part_sem, tile_sem = refs[n_parts + 1 + len(cuts) :]
    slots = held.shape[0]
    count = info[2 * slots]
    half = block // 2

    def tile_copy(k):
        return pltpu.make_async_copy(tiles.at[k], held.at[k], tile_sem.at[k])

    def begin(k, carry):
        tile_copy(k).start()
        return carry

    lax.fori_loop(0, count, begin, 0)
    started = []
    for i, (part, src, size, dst) in enumerate(copies):
        copy = pltpu.make_async_copy(
            parts[part].at[pl.ds(src, size)], panel.at[pl.ds(dst, size)], part_sem.at[i]
        )
        copy.start()
        started.append(copy)

    def clear(k, carry):
        at = pl.ds(pl.multiple_of(k * half, half), half)
        acc[at, :] = jnp.zeros((half, acc.shape[1]), F32)
        return carry

    lax.fori_loop(0, acc.shape[0] // half, clear, 0)
    for copy in started:
        copy.wait()

    def step(k, carry):
        tile_copy(k).wait()
        dst = pl.multiple_of(info[slots + k] * block, block)
        if transpose:
            src = pl.multiple_of(info[k] * half, half)
            low = panel[pl.ds(src, half), :]
            piece = jnp.concatenate([low, panel[pl.ds(src + panel.shape[0] // 2, half), :]], axis=0)
        else:
            piece = panel[pl.ds(pl.multiple_of(info[k] * block, block), block), :]
        for i in range(2):
            at = pl.ds(pl.multiple_of(dst + i * half, half), half)
            if transpose:
                left, dims = held[k, :, i * half : (i + 1) * half], (((0,), (0,)), ((), ()))
            else:
                left, dims = held[k, i * half : (i + 1) * half, :], (((1,), (0,)), ((), ()))
            acc[at, :] += lax.dot_general(left, piece, dims, preferred_element_type=F32)
        return carry

    lax.fori_loop(0, count, step, 0)
    for out, ranges in zip(outs, cuts):
        base = 0
        for start, rows in ranges:

            def give(k, carry, out=out, base=base, start=start):
                at = pl.multiple_of(k * half, half)
                out[pl.ds(base + at, half), :] = acc[pl.ds(start + at, half), :].astype(BF)
                return carry

            lax.fori_loop(0, rows // half, give, 0)
            base += rows


def tile_terms(info, parts, copies, tiles, cuts, transpose):
    slots, block = tiles.shape[0], tiles.shape[1]
    rows = sum(c[2] for c in copies)
    width = parts[0].shape[1]

    def kernel(*refs):
        tile_kernel(copies, cuts, len(parts), block, transpose, *refs)

    return pl.pallas_call(
        kernel,
        out_shape=[jax.ShapeDtypeStruct((sum(n for _, n in r), width), BF) for r in cuts],
        in_specs=[pl.BlockSpec(memory_space=pltpu.SMEM)]
        + [pl.BlockSpec(memory_space=pl.ANY)] * (len(parts) + 1),
        out_specs=[pl.BlockSpec(memory_space=pltpu.VMEM)] * len(cuts),
        scratch_shapes=[
            pltpu.VMEM((rows, width), BF),
            pltpu.VMEM((rows, width), F32),
            pltpu.VMEM((slots, block, block), BF),
            pltpu.SemaphoreType.DMA((len(copies),)),
            pltpu.SemaphoreType.DMA((slots,)),
        ],
        compiler_params=pltpu.CompilerParams(vmem_limit_bytes=VMEM_LIMIT),
        cost_estimate=pl.CostEstimate(
            flops=2 * slots * block * block * width,
            bytes_accessed=2 * slots * block * block + 4 * rows * width,
            transcendentals=0,
        ),
        name="tiles_t" if transpose else "tiles",
    )(info, *parts, tiles)


def node_kernel(s0, s1, s2, s3, s4, features, weight, cotangent, output, adjoint, m0, m1):
    rows = features.shape[0]
    half = rows // 2
    term = jnp.zeros(weight.shape, F32)
    for i, message in enumerate((m0, m1)):
        at = pl.ds(i * half, half)
        summed = add(s0[at, :], s1[at, :], s2[at, :]) + add(s3[at, :], s4[at, :])
        agg = (summed + features[at, :].astype(F32)).astype(BF)
        pre = jnp.dot(agg, weight[...], preferred_element_type=F32)
        sig = jax.nn.sigmoid(pre)
        output[at, :] = (pre * sig).astype(BF)
        slope = (cotangent[at, :].astype(F32) * sig * (1.0 + pre * (1.0 - sig))).astype(BF)
        back = lax.dot_general(
            slope, weight[...], (((1,), (1,)), ((), ())), preferred_element_type=F32
        ).astype(BF)
        adjoint[at, :] = back
        message[pl.ds(0, half), :] = back
        term = term + lax.dot_general(
            agg, slope, (((0,), (0,)), ((), ())), preferred_element_type=F32
        )
    wh = weight.shape[0] // 2
    m0[pl.ds(half, wh), :] = term[:wh].astype(BF)
    m1[pl.ds(half, wh), :] = term[wh:].astype(BF)


def node_step(sums, features, weight, cotangent):
    rows, width = features.shape
    message = jax.ShapeDtypeStruct(((rows + weight.shape[0]) // 2, width), BF)
    whole = jax.ShapeDtypeStruct((rows, width), BF)
    return pl.pallas_call(
        node_kernel,
        out_shape=[whole, whole, message, message],
        compiler_params=pltpu.CompilerParams(vmem_limit_bytes=16 * 1024 * 1024),
        cost_estimate=pl.CostEstimate(
            flops=6 * rows * width * width, bytes_accessed=20 * rows * width, transcendentals=rows * width
        ),
        name="nodes",
    )(*sums, features, weight, cotangent)


def row_place(cols, z, c, sign):
    return 2 * (((cols // 2 - z) * sign) % 8) + jnp.where(cols % 2 == c, 0, 1)


def gather_row(block):
    n = block.shape[0]
    other = send(block, core_move())
    parts = {0: block, 1: other}
    a, b = block, other
    for k in (1, 2, 3, 4):
        a = send(a, z_move())
        parts[2 * k] = a
        parts[2 * (8 - k) + 1] = send(a, core_move())
        if k < 4:
            b = send(b, z_move())
            parts[2 * k + 1] = b
            parts[2 * (8 - k)] = send(b, core_move())
    return [parts[i] for i in range(16)], [(i, 0, n, i * n) for i in range(16)]


def row_cuts(n):
    order = ((0,), (1,), (8,), (6,), (7,), (4,), (5,), (2,), (3,), (9,), (11, 10), (13, 12), (15, 14))
    return [[(i * n, n) for i in blocks] for blocks in order]


def scatter_row(outs, term, weight_term):
    own, other, far_own, a3, b3, a2, b2, a1, b1, give_4, give_3, give_2, give_1 = outs
    n = far_own.shape[0]
    wh = weight_term.shape[0] // 2
    got = [send(v, core_move()) for v in (give_4, give_3, give_2, give_1)]
    a = send(join([(n, [(0, 0), (1, 0)]), (wh, [(2, 0)])], far_own, got[0], weight_term), z_move())
    b = send(weight_term[wh:], z_move())
    held_a, held_b = [a], [b]
    for near_a, near_b, extra in ((a3, b3, got[1]), (a2, b2, got[2]), (a1, b1, got[3])):
        last = b.shape[0] - wh
        terms = [(0, 0), (1, n)] + ([(2, 0)] if last else [])
        sent_b = join([(n, terms), (wh, [(2, last)])], near_b, extra, b)
        terms = [(n, [(0, 0), (1, 0), (2, 0)]), (wh, [(2, n)])]
        sent_a = join(terms, near_a, extra, a, after=[sent_b])
        b, a = send(sent_b, z_move()), send(sent_a, z_move())
        held_a.append(a)
        held_b.append(b)
    back = send(join([(n, [(0, 0), (1, 0)])], other, b), core_move())
    rows = [(wh, [(i, v.shape[0] - wh)]) for i, v in enumerate(held_a[:3] + held_b[:3])]
    far = send(join(rows, *held_a[:3], *held_b[:3], after=[sent_a]), core_move())
    sums = []
    for h, held in ((0, held_a), (1, held_b)):
        w0 = weight_term[h * wh : (h + 1) * wh]
        m = [v[v.shape[0] - wh :] for v in held]
        s = [far[(3 * h + k) * wh : (3 * h + k + 1) * wh] for k in range(3)]
        sums.append((add(w0, m[3]) + add(m[1], s[1])) + (add(s[0], m[2]) + add(s[2], m[0])))
    return (add(own) + add(a[:n])) + (add(term) + add(back)), cat(*sums)


def scatter_plane(outs):
    a0, b0, c0, a1, b1, c1, a3, b3, c3, ab_up, ab_down, c_up, c_down = outs
    n = a0.shape[0]
    h = n // 2
    up, down = plane_move(0, 1), plane_move(0, -1)
    p, m = send(ab_up, up), send(ab_down, down)
    pa = send(cat(add(a1[:h], p[:h]).astype(BF), a1[h:], c_up), up)
    ma = send(cat(a3[:h], add(a3[h:], m[:h]).astype(BF), c_down), down)
    pb = send(cat(add(b1[:n], p[h:]).astype(BF), b1[n:]), up)
    mb = send(cat(b3[:n], add(b3[n:], m[h:]).astype(BF)), down)
    far_up = send(add(a0[:h], pa[:h], ma[:h]).astype(BF), plane_move(1, 1))
    far_down = send(add(a0[h:], pa[h:n], ma[h:n]).astype(BF), plane_move(1, -1))
    pc = send(cat(add(c1[:h], pa[n:]).astype(BF), c1[h:]), up)
    mc = send(cat(c3[:h], add(c3[h:], ma[n:]).astype(BF)), down)
    right = cat(
        add(b0[:h], pb[:h], mb[:h], far_up).astype(BF), add(b0[h:n], pb[h:n], mb[h:n]).astype(BF)
    )
    left = cat(
        add(b0[n : n + h], pb[n : n + h], mb[n : n + h]).astype(BF),
        add(b0[n + h :], pb[n + h :], mb[n + h :], far_down).astype(BF),
    )
    return [c0, pc, mc, send(right, plane_move(1, 1)), send(left, plane_move(1, -1))]


def plane_cuts(n):
    cuts = []
    for da in (0, 1, 3):
        cuts += [[(4 * da * n, n)], [((4 * da + 1) * n, 2 * n)], [((4 * da + 3) * n, n)]]
    h = n // 2
    cuts += [[(8 * n, h), (9 * n, n)], [(8 * n + h, h), (10 * n, n)]]
    return cuts + [[(11 * n, h)], [(11 * n + h, h)]]


def gather_plane(adjoint, messages):
    n = adjoint.shape[0]
    h = n // 2
    wh = messages[0].shape[0] - h
    parts, copies = [], []

    def ring(v, stage):
        m = v.shape[0] // 2
        up, down = plane_move(stage, 1), plane_move(stage, -1)
        r, l = send(v, up), send(v, down)
        return l, r, send(r[:m], up), send(l[m:], down)

    for i, v in enumerate(messages):
        l, r, f_u, f_d = ring(v, 1)
        g = f_u.shape[0]
        sums = [((0, h), (4, h - g)), ((2, h), (1, h))]
        whole = join(
            [(h, [(0, 0)]), (h, [(1, 0)]), (h, [(2, 0)]), (g, [(3, 0)]), (h - g, [(4, 0)]), (wh, sums)],
            v, l, r, f_u, f_d,
        )
        q_l, q_r, q_u, q_d = ring(whole, 0)
        m = q_u.shape[0]
        places = ((0, 4 * h, 0), (1, 4 * h, 4 * h), (2, 4 * h, 12 * h), (3, m, 8 * h), (4, 4 * h - m, 8 * h + m))
        copies += [(len(parts) + j, 0, size, 16 * h * i + to) for j, size, to in places]
        parts += [whole, q_l, q_r, q_u, q_d]
    k, at = 4 * h, 4 * h - m
    return parts, copies, join(
        [(wh, [((i, k), (i + 3, at)), ((i + 1, k), (i + 2, k))]) for i in (0, 4)],
        *[parts[i] for i in (0, 1, 2, 4, 5, 6, 7, 9)],
    )


def local(tile_values, tile_rows, tile_cols, tile_counts, features, weight, cotangent):
    tiles = tile_values[0, 0]
    rows, cols, count = tile_rows[0, 0], tile_cols[0, 0], tile_counts[0]
    n, width = features.shape
    scale = 1.0 / math.sqrt(n * 256)
    z, c, x, y = (lax.axis_index(a) for a in AXES)
    sign = 1 - 2 * c
    dx, dy = (rows // 4 - x) % 4, (rows % 4 - y) % 4
    da, db = jnp.where(c == 0, dx, dy), jnp.where(c == 0, dy, dx)
    db_place = jnp.where(db % 2 == 0, jnp.where(db == 0, 3, 0), jnp.where(db == 1, 1, 2))
    fwd = jnp.concatenate([row_place(cols, z, c, -sign), da * 4 + db_place, count])
    bwd = jnp.concatenate([da * 4 + (db ^ (db >> 1)), row_place(cols, z, c, sign), count])

    parts, copies = gather_row(features)
    sums = scatter_plane(tile_terms(fwd, parts, copies, tiles, plane_cuts(n), False))
    output, adjoint, *messages = node_step(sums, features, weight, cotangent)
    parts, copies, w = gather_plane(adjoint, messages)
    w = add(w, send(w, core_move())).astype(BF)
    outs = tile_terms(bwd, parts, copies, tiles, row_cuts(n), True)
    grad, w = scatter_row(outs, adjoint, w)
    return (output, grad.astype(BF), w * scale)


def solution(mesh):
    grid = Mesh(mesh.devices.reshape(SIZES), AXES)
    row, rep = ("z", "c"), ("x", "y")
    placed = (
        P(row, rep, None, None, None),
        P(row, rep, None),
        P(row, rep, None),
        P(row, rep),
        P(AXES, None),
        P(),
        P(AXES, None),
    )
    return jax.shard_map(
        local,
        mesh=grid,
        in_specs=placed,
        out_specs=(P(AXES, None), P(AXES, None), P()),
        check_vma=False,
    )
```

```python
import math

import jax
import jax.numpy as jnp
from jax import lax
from jax.experimental import pallas as pl
from jax.experimental.pallas import tpu as pltpu
from jax.sharding import Mesh
from jax.sharding import PartitionSpec as P

AXES = ("z", "c", "x", "y")
SIZES = (8, 2, 4, 4)
BF = jnp.bfloat16
F32 = jnp.float32
VMEM_LIMIT = 44 * 1024 * 1024


def rank(q):
    out = 0
    for v, s in zip(q, SIZES):
        out = out * s + v
    return out


def pairs(move):
    z, c, x, y = SIZES
    every = [(i, j, k, l) for i in range(z) for j in range(c) for k in range(x) for l in range(y)]
    return [(rank(q), rank(move(q))) for q in every]


def z_move():
    return pairs(lambda q: ((q[0] + 1 - 2 * q[1]) % 8, q[1], q[2], q[3]))


def core_move():
    return pairs(lambda q: (q[0], 1 - q[1], q[2], q[3]))


def plane_move(stage, d):
    def move(q):
        z, c, x, y = q
        if (c == 0) == (stage == 0):
            return (z, c, (x + d) % 4, y)
        return (z, c, x, (y + d) % 4)

    return pairs(move)


def send(v, perm):
    return lax.ppermute(v, AXES, perm)


def add(*parts):
    total = parts[0].astype(F32)
    for p in parts[1:]:
        total = total + p.astype(F32)
    return total


def join(segments, *arrays, after=()):
    width = arrays[0].shape[1]

    def total(refs, terms, rows):
        picked = []
        for i, at in terms:
            if isinstance(i, tuple):
                picked.append(total(refs, (i, at), rows))
            else:
                picked.append(refs[i][at : at + rows, :])
        return picked[0] if len(picked) == 1 else add(*picked)

    def kernel(*refs):
        out = refs[-1]
        base = 0
        for rows, terms in segments:
            out[base : base + rows, :] = total(refs, terms, rows).astype(BF)
            base += rows

    rows = sum(r for r, _ in segments)
    return pl.pallas_call(
        kernel,
        out_shape=jax.ShapeDtypeStruct((rows, width), BF),
        in_specs=[pl.BlockSpec(memory_space=pltpu.VMEM)] * len(arrays)
        + [pl.BlockSpec(memory_space=pl.ANY)] * len(after),
        out_specs=pl.BlockSpec(memory_space=pltpu.VMEM),
        compiler_params=pltpu.CompilerParams(vmem_limit_bytes=16 * 1024 * 1024),
        cost_estimate=pl.CostEstimate(flops=rows, bytes_accessed=rows, transcendentals=0),
        name="join",
    )(*arrays, *after)


def tile_kernel(copies, cuts, n_parts, block, transpose, info, *refs):
    parts, tiles, outs = refs[:n_parts], refs[n_parts], refs[n_parts + 1 : n_parts + 1 + len(cuts)]
    panel, acc, held, part_sem, tile_sem = refs[n_parts + 1 + len(cuts) :]
    slots = held.shape[0]
    count = info[2 * slots]
    half = block // 2

    def tile_copy(k):
        return pltpu.make_async_copy(tiles.at[k], held.at[k], tile_sem.at[k])

    def begin(k, carry):
        tile_copy(k).start()
        return carry

    lax.fori_loop(0, count, begin, 0)
    started = []
    for i, (part, src, size, dst) in enumerate(copies):
        copy = pltpu.make_async_copy(
            parts[part].at[pl.ds(src, size)], panel.at[pl.ds(dst, size)], part_sem.at[i]
        )
        copy.start()
        started.append(copy)

    def clear(k, carry):
        at = pl.ds(pl.multiple_of(k * half, half), half)
        acc[at, :] = jnp.zeros((half, acc.shape[1]), F32)
        return carry

    lax.fori_loop(0, acc.shape[0] // half, clear, 0)
    for copy in started:
        copy.wait()

    def step(k, carry):
        tile_copy(k).wait()
        dst = pl.multiple_of(info[slots + k] * block, block)
        if transpose:
            src = pl.multiple_of(info[k] * half, half)
            low = panel[pl.ds(src, half), :]
            piece = jnp.concatenate([low, panel[pl.ds(src + panel.shape[0] // 2, half), :]], axis=0)
        else:
            piece = panel[pl.ds(pl.multiple_of(info[k] * block, block), block), :]
        for i in range(2):
            at = pl.ds(pl.multiple_of(dst + i * half, half), half)
            if transpose:
                left, dims = held[k, :, i * half : (i + 1) * half], (((0,), (0,)), ((), ()))
            else:
                left, dims = held[k, i * half : (i + 1) * half, :], (((1,), (0,)), ((), ()))
            acc[at, :] += lax.dot_general(left, piece, dims, preferred_element_type=F32)
        return carry

    lax.fori_loop(0, count, step, 0)
    for out, ranges in zip(outs, cuts):
        base = 0
        for start, rows in ranges:

            def give(k, carry, out=out, base=base, start=start):
                at = pl.multiple_of(k * half, half)
                out[pl.ds(base + at, half), :] = acc[pl.ds(start + at, half), :].astype(BF)
                return carry

            lax.fori_loop(0, rows // half, give, 0)
            base += rows


def tile_terms(info, parts, copies, tiles, cuts, transpose):
    slots, block = tiles.shape[0], tiles.shape[1]
    rows = sum(c[2] for c in copies)
    width = parts[0].shape[1]

    def kernel(*refs):
        tile_kernel(copies, cuts, len(parts), block, transpose, *refs)

    return pl.pallas_call(
        kernel,
        out_shape=[jax.ShapeDtypeStruct((sum(n for _, n in r), width), BF) for r in cuts],
        in_specs=[pl.BlockSpec(memory_space=pltpu.SMEM)]
        + [pl.BlockSpec(memory_space=pl.ANY)] * (len(parts) + 1),
        out_specs=[pl.BlockSpec(memory_space=pltpu.VMEM)] * len(cuts),
        scratch_shapes=[
            pltpu.VMEM((rows, width), BF),
            pltpu.VMEM((rows, width), F32),
            pltpu.VMEM((slots, block, block), BF),
            pltpu.SemaphoreType.DMA((len(copies),)),
            pltpu.SemaphoreType.DMA((slots,)),
        ],
        compiler_params=pltpu.CompilerParams(vmem_limit_bytes=VMEM_LIMIT),
        cost_estimate=pl.CostEstimate(
            flops=2 * slots * block * block * width,
            bytes_accessed=2 * slots * block * block + 4 * rows * width,
            transcendentals=0,
        ),
        name="tiles_t" if transpose else "tiles",
    )(info, *parts, tiles)


def node_kernel(s0, s1, s2, s3, s4, features, weight, cotangent, output, adjoint, m0, m1):
    rows = features.shape[0]
    half = rows // 2
    term = jnp.zeros(weight.shape, F32)
    for i, message in enumerate((m0, m1)):
        at = pl.ds(i * half, half)
        summed = add(s0[at, :], s1[at, :], s2[at, :]) + add(s3[at, :], s4[at, :])
        agg = (summed + features[at, :].astype(F32)).astype(BF)
        pre = jnp.dot(agg, weight[...], preferred_element_type=F32)
        sig = jax.nn.sigmoid(pre)
        output[at, :] = (pre * sig).astype(BF)
        slope = (cotangent[at, :].astype(F32) * sig * (1.0 + pre * (1.0 - sig))).astype(BF)
        back = lax.dot_general(
            slope, weight[...], (((1,), (1,)), ((), ())), preferred_element_type=F32
        ).astype(BF)
        adjoint[at, :] = back
        message[pl.ds(0, half), :] = back
        term = term + lax.dot_general(
            agg, slope, (((0,), (0,)), ((), ())), preferred_element_type=F32
        )
    wh = weight.shape[0] // 2
    m0[pl.ds(half, wh), :] = term[:wh].astype(BF)
    m1[pl.ds(half, wh), :] = term[wh:].astype(BF)


def node_step(sums, features, weight, cotangent):
    rows, width = features.shape
    message = jax.ShapeDtypeStruct(((rows + weight.shape[0]) // 2, width), BF)
    whole = jax.ShapeDtypeStruct((rows, width), BF)
    return pl.pallas_call(
        node_kernel,
        out_shape=[whole, whole, message, message],
        compiler_params=pltpu.CompilerParams(vmem_limit_bytes=16 * 1024 * 1024),
        cost_estimate=pl.CostEstimate(
            flops=6 * rows * width * width, bytes_accessed=20 * rows * width, transcendentals=rows * width
        ),
        name="nodes",
    )(*sums, features, weight, cotangent)


def row_place(cols, z, c, sign):
    return 2 * (((cols // 2 - z) * sign) % 8) + jnp.where(cols % 2 == c, 0, 1)


def gather_row(block):
    n = block.shape[0]
    other = send(block, core_move())
    parts = {0: block, 1: other}
    a, b = block, other
    for k in (1, 2, 3, 4):
        a = send(a, z_move())
        parts[2 * k] = a
        parts[2 * (8 - k) + 1] = send(a, core_move())
        if k < 4:
            b = send(b, z_move())
            parts[2 * k + 1] = b
            parts[2 * (8 - k)] = send(b, core_move())
    return [parts[i] for i in range(16)], [(i, 0, n, i * n) for i in range(16)]


def row_cuts(n):
    order = ((0,), (1,), (8,), (6,), (7,), (4,), (5,), (2,), (3,), (9,), (11, 10), (13, 12), (15, 14))
    return [[(i * n, n) for i in blocks] for blocks in order]


def scatter_row(outs, term, weight_term):
    own, other, far_own, a3, b3, a2, b2, a1, b1, give_4, give_3, give_2, give_1 = outs
    n = far_own.shape[0]
    wh = weight_term.shape[0] // 2
    got = [send(v, core_move()) for v in (give_4, give_3, give_2, give_1)]
    a = send(join([(n, [(0, 0), (1, 0)]), (wh, [(2, 0)])], far_own, got[0], weight_term), z_move())
    b = send(weight_term[wh:], z_move())
    held_a, held_b = [a], [b]
    for near_a, near_b, extra in ((a3, b3, got[1]), (a2, b2, got[2]), (a1, b1, got[3])):
        last = b.shape[0] - wh
        terms = [(0, 0), (1, n)] + ([(2, 0)] if last else [])
        sent_b = join([(n, terms), (wh, [(2, last)])], near_b, extra, b)
        terms = [(n, [(0, 0), (1, 0), (2, 0)]), (wh, [(2, n)])]
        sent_a = join(terms, near_a, extra, a, after=[sent_b])
        b, a = send(sent_b, z_move()), send(sent_a, z_move())
        held_a.append(a)
        held_b.append(b)
    back = send(join([(n, [(0, 0), (1, 0)])], other, b), core_move())
    rows = [(wh, [(i, v.shape[0] - wh)]) for i, v in enumerate(held_a[:3] + held_b[:3])]
    far = send(join(rows, *held_a[:3], *held_b[:3], after=[sent_a]), core_move())
    return last_step(own, a, term, back, weight_term, far, held_a, held_b)


def last_step(own, a, term, back, weight_term, far, held_a, held_b):
    n, width = own.shape
    wh = weight_term.shape[0] // 2
    scale = 1.0 / math.sqrt(n * 256)

    def kernel(*refs):
        own, a, term, back, w, far, *held = refs[:-2]
        grad, weight = refs[-2:]
        grad[...] = (
            (add(own[...]) + add(a[:n, :])) + (add(term[...]) + add(back[...]))
        ).astype(BF)
        for h in (0, 1):
            m = [r[r.shape[0] - wh :, :] for r in held[4 * h : 4 * h + 4]]
            s = [far[(3 * h + k) * wh : (3 * h + k + 1) * wh, :] for k in range(3)]
            even = add(w[h * wh : (h + 1) * wh, :], m[3]) + add(m[1], s[1])
            odd = add(s[0], m[2]) + add(s[2], m[0])
            weight[h * wh : (h + 1) * wh, :] = (even + odd) * scale

    return pl.pallas_call(
        kernel,
        out_shape=[
            jax.ShapeDtypeStruct((n, width), BF),
            jax.ShapeDtypeStruct((2 * wh, width), F32),
        ],
        compiler_params=pltpu.CompilerParams(vmem_limit_bytes=16 * 1024 * 1024),
        cost_estimate=pl.CostEstimate(flops=n, bytes_accessed=n, transcendentals=0),
        name="last",
    )(own, a, term, back, weight_term, far, *held_a, *held_b)


def scatter_plane(outs):
    a0, b0, c0, a1, b1, c1, a3, b3, c3, ab_up, ab_down, c_up, c_down = outs
    n = a0.shape[0]
    h = n // 2
    up, down = plane_move(0, 1), plane_move(0, -1)
    p, m = send(ab_up, up), send(ab_down, down)
    pa = send(join([(h, [(0, 0), (1, 0)]), (h, [(0, h)]), (h, [(2, 0)])], a1, p, c_up), up)
    ma = send(join([(h, [(0, 0)]), (h, [(0, h), (1, 0)]), (h, [(2, 0)])], a3, m, c_down), down)
    pb = send(join([(n, [(0, 0), (1, h)]), (n, [(0, n)])], b1, p), up)
    mb = send(join([(n, [(0, 0)]), (n, [(0, n), (1, h)])], b3, m), down)
    far_up = send(join([(h, [(i, 0) for i in range(3)])], a0, pa, ma), plane_move(1, 1))
    far_down = send(join([(h, [(i, h) for i in range(3)])], a0, pa, ma), plane_move(1, -1))
    pc = send(join([(h, [(0, 0), (1, n)]), (h, [(0, h)])], c1, pa), up)
    mc = send(join([(h, [(0, 0)]), (h, [(0, h), (1, n)])], c3, ma), down)
    near, far = [(i, 0) for i in range(4)], [(i, h) for i in range(3)]
    right = join([(h, near), (h, far)], b0, pb, mb, far_up)
    near, far = [(i, n) for i in range(3)], [(i, n + h) for i in range(3)] + [(3, 0)]
    left = join([(h, near), (h, far)], b0, pb, mb, far_down)
    return [c0, pc, mc, send(right, plane_move(1, 1)), send(left, plane_move(1, -1))]


def plane_cuts(n):
    cuts = []
    for da in (0, 1, 3):
        cuts += [[(4 * da * n, n)], [((4 * da + 1) * n, 2 * n)], [((4 * da + 3) * n, n)]]
    h = n // 2
    cuts += [[(8 * n, h), (9 * n, n)], [(8 * n + h, h), (10 * n, n)]]
    return cuts + [[(11 * n, h)], [(11 * n + h, h)]]


def gather_plane(adjoint, messages):
    n = adjoint.shape[0]
    h = n // 2
    wh = messages[0].shape[0] - h
    parts, copies = [], []

    def ring(v, stage):
        m = v.shape[0] // 2
        up, down = plane_move(stage, 1), plane_move(stage, -1)
        r, l = send(v, up), send(v, down)
        return l, r, send(r[:m], up), send(l[m:], down)

    for i, v in enumerate(messages):
        l, r, f_u, f_d = ring(v, 1)
        g = f_u.shape[0]
        sums = [((0, h), (4, h - g)), ((2, h), (1, h))]
        whole = join(
            [(h, [(0, 0)]), (h, [(1, 0)]), (h, [(2, 0)]), (g, [(3, 0)]), (h - g, [(4, 0)]), (wh, sums)],
            v, l, r, f_u, f_d,
        )
        q_l, q_r, q_u, q_d = ring(whole, 0)
        m = q_u.shape[0]
        places = ((0, 4 * h, 0), (1, 4 * h, 4 * h), (2, 4 * h, 12 * h), (3, m, 8 * h), (4, 4 * h - m, 8 * h + m))
        copies += [(len(parts) + j, 0, size, 16 * h * i + to) for j, size, to in places]
        parts += [whole, q_l, q_r, q_u, q_d]
    k, at = 4 * h, 4 * h - m
    return parts, copies, join(
        [(wh, [((i, k), (i + 3, at)), ((i + 1, k), (i + 2, k))]) for i in (0, 4)],
        *[parts[i] for i in (0, 1, 2, 4, 5, 6, 7, 9)],
    )


def local(tile_values, tile_rows, tile_cols, tile_counts, features, weight, cotangent):
    tiles = tile_values[0, 0]
    rows, cols, count = tile_rows[0, 0], tile_cols[0, 0], tile_counts[0]
    n, width = features.shape
    z, c, x, y = (lax.axis_index(a) for a in AXES)
    sign = 1 - 2 * c
    dx, dy = (rows // 4 - x) % 4, (rows % 4 - y) % 4
    da, db = jnp.where(c == 0, dx, dy), jnp.where(c == 0, dy, dx)
    db_place = jnp.where(db % 2 == 0, jnp.where(db == 0, 3, 0), jnp.where(db == 1, 1, 2))
    fwd = jnp.concatenate([row_place(cols, z, c, -sign), da * 4 + db_place, count])
    bwd = jnp.concatenate([da * 4 + (db ^ (db >> 1)), row_place(cols, z, c, sign), count])

    parts, copies = gather_row(features)
    sums = scatter_plane(tile_terms(fwd, parts, copies, tiles, plane_cuts(n), False))
    output, adjoint, *messages = node_step(sums, features, weight, cotangent)
    parts, copies, w = gather_plane(adjoint, messages)
    w = join([(w.shape[0], [(0, 0), (1, 0)])], w, send(w, core_move()))
    outs = tile_terms(bwd, parts, copies, tiles, row_cuts(n), True)
    grad, w = scatter_row(outs, adjoint, w)
    return (output, grad, w)


def solution(mesh):
    grid = Mesh(mesh.devices.reshape(SIZES), AXES)
    row, rep = ("z", "c"), ("x", "y")
    placed = (
        P(row, rep, None, None, None),
        P(row, rep, None),
        P(row, rep, None),
        P(row, rep),
        P(AXES, None),
        P(),
        P(AXES, None),
    )
    return jax.shard_map(
        local,
        mesh=grid,
        in_specs=placed,
        out_specs=(P(AXES, None), P(AXES, None), P()),
        check_vma=False,
    )
```

```python
import math

import jax
import jax.numpy as jnp
from jax import lax
from jax.experimental import pallas as pl
from jax.experimental.pallas import tpu as pltpu
from jax.sharding import Mesh
from jax.sharding import PartitionSpec as P

AXES = ("z", "c", "x", "y")
SIZES = (8, 2, 4, 4)
BF = jnp.bfloat16
F32 = jnp.float32
VMEM_LIMIT = 44 * 1024 * 1024


def rank(q):
    out = 0
    for v, s in zip(q, SIZES):
        out = out * s + v
    return out


def pairs(move):
    z, c, x, y = SIZES
    every = [(i, j, k, l) for i in range(z) for j in range(c) for k in range(x) for l in range(y)]
    return [(rank(q), rank(move(q))) for q in every]


def z_move():
    return pairs(lambda q: ((q[0] + 1 - 2 * q[1]) % 8, q[1], q[2], q[3]))


def core_move():
    return pairs(lambda q: (q[0], 1 - q[1], q[2], q[3]))


def plane_move(stage, d):
    def move(q):
        z, c, x, y = q
        if (c == 0) == (stage == 0):
            return (z, c, (x + d) % 4, y)
        return (z, c, x, (y + d) % 4)

    return pairs(move)


def send(v, perm):
    return lax.ppermute(v, AXES, perm)


def add(*parts):
    total = parts[0].astype(F32)
    for p in parts[1:]:
        total = total + p.astype(F32)
    return total


def join(segments, *arrays, after=()):
    width = arrays[0].shape[1]

    def total(refs, terms, rows):
        picked = []
        for i, at in terms:
            if isinstance(i, tuple):
                picked.append(total(refs, (i, at), rows))
            else:
                picked.append(refs[i][at : at + rows, :])
        return picked[0] if len(picked) == 1 else add(*picked)

    def kernel(*refs):
        out = refs[-1]
        base = 0
        for rows, terms in segments:
            out[base : base + rows, :] = total(refs, terms, rows).astype(BF)
            base += rows

    rows = sum(r for r, _ in segments)
    return pl.pallas_call(
        kernel,
        out_shape=jax.ShapeDtypeStruct((rows, width), BF),
        in_specs=[pl.BlockSpec(memory_space=pltpu.VMEM)] * len(arrays)
        + [pl.BlockSpec(memory_space=pl.ANY)] * len(after),
        out_specs=pl.BlockSpec(memory_space=pltpu.VMEM),
        compiler_params=pltpu.CompilerParams(vmem_limit_bytes=16 * 1024 * 1024),
        cost_estimate=pl.CostEstimate(flops=rows, bytes_accessed=rows, transcendentals=0),
        name="join",
    )(*arrays, *after)


def tile_kernel(copies, cuts, n_parts, block, transpose, info, *refs):
    parts, tiles, outs = refs[:n_parts], refs[n_parts], refs[n_parts + 1 : n_parts + 1 + len(cuts)]
    panel, acc, held, part_sem, tile_sem = refs[n_parts + 1 + len(cuts) :]
    slots = held.shape[0]
    count = info[2 * slots]
    half = block // 2

    def tile_copy(k):
        return pltpu.make_async_copy(tiles.at[k], held.at[k], tile_sem.at[k])

    def begin(k, carry):
        tile_copy(k).start()
        return carry

    lax.fori_loop(0, count, begin, 0)
    started = []
    for i, (part, src, size, dst) in enumerate(copies):
        copy = pltpu.make_async_copy(
            parts[part].at[pl.ds(src, size)], panel.at[pl.ds(dst, size)], part_sem.at[i]
        )
        copy.start()
        started.append(copy)

    def clear(k, carry):
        at = pl.ds(pl.multiple_of(k * half, half), half)
        acc[at, :] = jnp.zeros((half, acc.shape[1]), F32)
        return carry

    lax.fori_loop(0, acc.shape[0] // half, clear, 0)
    for copy in started:
        copy.wait()

    def step(k, carry):
        tile_copy(k).wait()
        dst = pl.multiple_of(info[slots + k] * block, block)
        if transpose:
            src = pl.multiple_of(info[k] * half, half)
            low = panel[pl.ds(src, half), :]
            piece = jnp.concatenate([low, panel[pl.ds(src + panel.shape[0] // 2, half), :]], axis=0)
        else:
            piece = panel[pl.ds(pl.multiple_of(info[k] * block, block), block), :]
        for i in range(2):
            at = pl.ds(pl.multiple_of(dst + i * half, half), half)
            if transpose:
                left, dims = held[k, :, i * half : (i + 1) * half], (((0,), (0,)), ((), ()))
            else:
                left, dims = held[k, i * half : (i + 1) * half, :], (((1,), (0,)), ((), ()))
            acc[at, :] += lax.dot_general(left, piece, dims, preferred_element_type=F32)
        return carry

    lax.fori_loop(0, count, step, 0)
    for out, ranges in zip(outs, cuts):
        base = 0
        for start, rows in ranges:

            def give(k, carry, out=out, base=base, start=start):
                at = pl.multiple_of(k * half, half)
                out[pl.ds(base + at, half), :] = acc[pl.ds(start + at, half), :].astype(BF)
                return carry

            lax.fori_loop(0, rows // half, give, 0)
            base += rows


def tile_terms(info, parts, copies, tiles, cuts, transpose):
    slots, block = tiles.shape[0], tiles.shape[1]
    rows = sum(c[2] for c in copies)
    width = parts[0].shape[1]

    def kernel(*refs):
        tile_kernel(copies, cuts, len(parts), block, transpose, *refs)

    return pl.pallas_call(
        kernel,
        out_shape=[jax.ShapeDtypeStruct((sum(n for _, n in r), width), BF) for r in cuts],
        in_specs=[pl.BlockSpec(memory_space=pltpu.SMEM)]
        + [pl.BlockSpec(memory_space=pl.ANY)] * (len(parts) + 1),
        out_specs=[pl.BlockSpec(memory_space=pltpu.VMEM)] * len(cuts),
        scratch_shapes=[
            pltpu.VMEM((rows, width), BF),
            pltpu.VMEM((rows, width), F32),
            pltpu.VMEM((slots, block, block), BF),
            pltpu.SemaphoreType.DMA((len(copies),)),
            pltpu.SemaphoreType.DMA((slots,)),
        ],
        compiler_params=pltpu.CompilerParams(vmem_limit_bytes=VMEM_LIMIT),
        cost_estimate=pl.CostEstimate(
            flops=2 * slots * block * block * width,
            bytes_accessed=2 * slots * block * block + 4 * rows * width,
            transcendentals=0,
        ),
        name="tiles_t" if transpose else "tiles",
    )(info, *parts, tiles)


def node_kernel(s0, s1, s2, s3, s4, features, weight, cotangent, output, adjoint, m0, m1):
    rows = features.shape[0]
    half = rows // 2
    term = jnp.zeros(weight.shape, F32)
    for i, message in enumerate((m0, m1)):
        at = pl.ds(i * half, half)
        summed = add(s0[at, :], s1[at, :], s2[at, :]) + add(s3[at, :], s4[at, :])
        agg = (summed + features[at, :].astype(F32)).astype(BF)
        pre = jnp.dot(agg, weight[...], preferred_element_type=F32)
        sig = jax.nn.sigmoid(pre)
        output[at, :] = (pre * sig).astype(BF)
        slope = (cotangent[at, :].astype(F32) * sig * (1.0 + pre * (1.0 - sig))).astype(BF)
        back = lax.dot_general(
            slope, weight[...], (((1,), (1,)), ((), ())), preferred_element_type=F32
        ).astype(BF)
        adjoint[at, :] = back
        message[pl.ds(0, half), :] = back
        term = term + lax.dot_general(
            agg, slope, (((0,), (0,)), ((), ())), preferred_element_type=F32
        )
    wh = weight.shape[0] // 2
    m0[pl.ds(half, wh), :] = term[:wh].astype(BF)
    m1[pl.ds(half, wh), :] = term[wh:].astype(BF)


def node_step(sums, features, weight, cotangent):
    rows, width = features.shape
    message = jax.ShapeDtypeStruct(((rows + weight.shape[0]) // 2, width), BF)
    whole = jax.ShapeDtypeStruct((rows, width), BF)
    return pl.pallas_call(
        node_kernel,
        out_shape=[whole, whole, message, message],
        compiler_params=pltpu.CompilerParams(vmem_limit_bytes=16 * 1024 * 1024),
        cost_estimate=pl.CostEstimate(
            flops=6 * rows * width * width, bytes_accessed=20 * rows * width, transcendentals=rows * width
        ),
        name="nodes",
    )(*sums, features, weight, cotangent)


def row_place(cols, z, c, sign):
    return 2 * (((cols // 2 - z) * sign) % 8) + jnp.where(cols % 2 == c, 0, 1)


def gather_row(block):
    n = block.shape[0]
    other = send(block, core_move())
    own = join([(n, [(0, 0)])], block)
    parts = {0: own, 1: other}
    a, b = block, other
    for k in (1, 2, 3, 4):
        a = send(a, z_move())
        parts[2 * k] = a
        parts[2 * (8 - k) + 1] = send(a, core_move())
        if k < 4:
            b = send(join([(n, [(0, 0)])], b, after=[own]) if k == 2 else b, z_move())
            parts[2 * k + 1] = b
            parts[2 * (8 - k)] = send(b, core_move())
    return [parts[i] for i in range(16)], [(i, 0, n, i * n) for i in range(16)]


def row_cuts(n):
    order = ((0,), (1,), (8,), (9,), (6,), (7,), (4,), (5,), (2,), (3,), (11, 10), (13, 12), (15, 14))
    return [[(i * n, n) for i in blocks] for blocks in order]


def scatter_row(outs, term, weight_term):
    own, other, a4, b4, a3, b3, a2, b2, a1, b1, give_3, give_2, give_1 = outs
    n = own.shape[0]
    wh = weight_term.shape[0] // 2
    got = [send(v, core_move()) for v in (give_3, give_2, give_1)]
    a = send(join([(n, [(0, 0)]), (wh, [(1, 0)])], a4, weight_term), z_move())
    b = send(join([(n, [(0, 0)]), (wh, [(1, wh)])], b4, weight_term), z_move())
    held_a, held_b = [a], [b]
    for near_a, near_b, extra in ((a3, b3, got[0]), (a2, b2, got[1]), (a1, b1, got[2])):
        sent_b = join([(n, [(0, 0), (1, n), (2, 0)]), (wh, [(2, n)])], near_b, extra, b)
        terms = [(n, [(0, 0), (1, 0), (2, 0)]), (wh, [(2, n)])]
        sent_a = join(terms, near_a, extra, a, after=[sent_b])
        b, a = send(sent_b, z_move()), send(sent_a, z_move())
        held_a.append(a)
        held_b.append(b)
    back = send(join([(n, [(0, 0), (1, 0)])], other, b), core_move())
    rows = [(wh, [(i, n)]) for i in range(6)]
    far = send(join(rows, *held_a[:3], *held_b[:3], after=[sent_a]), core_move())
    return last_step(own, a, term, back, weight_term, far, held_a, held_b)


def last_step(own, a, term, back, weight_term, far, held_a, held_b):
    n, width = own.shape
    wh = weight_term.shape[0] // 2
    scale = 1.0 / math.sqrt(n * 256)

    def kernel(*refs):
        own, a, term, back, w, far, *held = refs[:-2]
        grad, weight = refs[-2:]
        grad[...] = (
            (add(own[...]) + add(a[:n, :])) + (add(term[...]) + add(back[...]))
        ).astype(BF)
        for h in (0, 1):
            m = [r[n:, :] for r in held[4 * h : 4 * h + 4]]
            s = [far[(3 * h + k) * wh : (3 * h + k + 1) * wh, :] for k in range(3)]
            even = add(w[h * wh : (h + 1) * wh, :], m[3]) + add(m[1], s[1])
            odd = add(s[0], m[2]) + add(s[2], m[0])
            weight[h * wh : (h + 1) * wh, :] = (even + odd) * scale

    return pl.pallas_call(
        kernel,
        out_shape=[
            jax.ShapeDtypeStruct((n, width), BF),
            jax.ShapeDtypeStruct((2 * wh, width), F32),
        ],
        compiler_params=pltpu.CompilerParams(vmem_limit_bytes=16 * 1024 * 1024),
        cost_estimate=pl.CostEstimate(flops=n, bytes_accessed=n, transcendentals=0),
        name="last",
    )(own, a, term, back, weight_term, far, *held_a, *held_b)


def scatter_plane(outs):
    a0, b0, c0, a1, b1, c1, a3, b3, c3, ab_up, ab_down, c_up, c_down = outs
    n = a0.shape[0]
    h = n // 2
    up, down = plane_move(0, 1), plane_move(0, -1)
    p, m = send(ab_up, up), send(ab_down, down)
    pa = send(join([(h, [(0, 0), (1, 0)]), (h, [(0, h)]), (h, [(2, 0)])], a1, p, c_up), up)
    ma = send(join([(h, [(0, 0)]), (h, [(0, h), (1, 0)]), (h, [(2, 0)])], a3, m, c_down), down)
    pb = send(join([(n, [(0, 0), (1, h)]), (n, [(0, n)])], b1, p), up)
    mb = send(join([(n, [(0, 0)]), (n, [(0, n), (1, h)])], b3, m), down)
    far_up = send(join([(h, [(i, 0) for i in range(3)])], a0, pa, ma), plane_move(1, 1))
    far_down = send(join([(h, [(i, h) for i in range(3)])], a0, pa, ma), plane_move(1, -1))
    pc = send(join([(h, [(0, 0), (1, n)]), (h, [(0, h)])], c1, pa), up)
    mc = send(join([(h, [(0, 0)]), (h, [(0, h), (1, n)])], c3, ma), down)
    near, far = [(i, 0) for i in range(4)], [(i, h) for i in range(3)]
    right = join([(h, near), (h, far)], b0, pb, mb, far_up)
    near, far = [(i, n) for i in range(3)], [(i, n + h) for i in range(3)] + [(3, 0)]
    left = join([(h, near), (h, far)], b0, pb, mb, far_down)
    return [c0, pc, mc, send(right, plane_move(1, 1)), send(left, plane_move(1, -1))]


def plane_cuts(n):
    cuts = []
    for da in (0, 1, 3):
        cuts += [[(4 * da * n, n)], [((4 * da + 1) * n, 2 * n)], [((4 * da + 3) * n, n)]]
    h = n // 2
    cuts += [[(8 * n, h), (9 * n, n)], [(8 * n + h, h), (10 * n, n)]]
    return cuts + [[(11 * n, h)], [(11 * n + h, h)]]


def gather_plane(adjoint, messages):
    n = adjoint.shape[0]
    h = n // 2
    wh = messages[0].shape[0] - h
    parts, copies = [], []

    def ring(v, stage):
        m = v.shape[0] // 2
        up, down = plane_move(stage, 1), plane_move(stage, -1)
        r, l = send(v, up), send(v, down)
        return l, r, send(r[:m], up), send(l[m:], down)

    for i, v in enumerate(messages):
        l, r, f_u, f_d = ring(v, 1)
        g = f_u.shape[0]
        sums = [((0, h), (4, h - g)), ((2, h), (1, h))]
        whole = join(
            [(h, [(0, 0)]), (h, [(1, 0)]), (h, [(2, 0)]), (g, [(3, 0)]), (h - g, [(4, 0)]), (wh, sums)],
            v, l, r, f_u, f_d,
        )
        q_l, q_r, q_u, q_d = ring(whole, 0)
        m = q_u.shape[0]
        places = ((0, 4 * h, 0), (1, 4 * h, 4 * h), (2, 4 * h, 12 * h), (3, m, 8 * h), (4, 4 * h - m, 8 * h + m))
        copies += [(len(parts) + j, 0, size, 16 * h * i + to) for j, size, to in places]
        parts += [whole, q_l, q_r, q_u, q_d]
    k, at = 4 * h, 4 * h - m
    return parts, copies, join(
        [(wh, [((i, k), (i + 3, at)), ((i + 1, k), (i + 2, k))]) for i in (0, 4)],
        *[parts[i] for i in (0, 1, 2, 4, 5, 6, 7, 9)],
    )


def local(tile_values, tile_rows, tile_cols, tile_counts, features, weight, cotangent):
    tiles = tile_values[0, 0]
    rows, cols, count = tile_rows[0, 0], tile_cols[0, 0], tile_counts[0]
    n, width = features.shape
    z, c, x, y = (lax.axis_index(a) for a in AXES)
    sign = 1 - 2 * c
    dx, dy = (rows // 4 - x) % 4, (rows % 4 - y) % 4
    da, db = jnp.where(c == 0, dx, dy), jnp.where(c == 0, dy, dx)
    db_place = jnp.where(db % 2 == 0, jnp.where(db == 0, 3, 0), jnp.where(db == 1, 1, 2))
    fwd = jnp.concatenate([row_place(cols, z, c, -sign), da * 4 + db_place, count])
    bwd = jnp.concatenate([da * 4 + (db ^ (db >> 1)), row_place(cols, z, c, sign), count])

    parts, copies = gather_row(features)
    sums = scatter_plane(tile_terms(fwd, parts, copies, tiles, plane_cuts(n), False))
    output, adjoint, *messages = node_step(sums, features, weight, cotangent)
    parts, copies, w = gather_plane(adjoint, messages)
    w = join([(w.shape[0], [(0, 0), (1, 0)])], w, send(w, core_move()))
    outs = tile_terms(bwd, parts, copies, tiles, row_cuts(n), True)
    grad, w = scatter_row(outs, adjoint, w)
    return (output, grad, w)


def solution(mesh):
    grid = Mesh(mesh.devices.reshape(SIZES), AXES)
    row, rep = ("z", "c"), ("x", "y")
    placed = (
        P(row, rep, None, None, None),
        P(row, rep, None),
        P(row, rep, None),
        P(row, rep),
        P(AXES, None),
        P(),
        P(AXES, None),
    )
    return jax.shard_map(
        local,
        mesh=grid,
        in_specs=placed,
        out_specs=(P(AXES, None), P(AXES, None), P()),
        check_vma=False,
    )
```

```python
import math

import jax
import jax.numpy as jnp
from jax import lax
from jax.experimental import pallas as pl
from jax.experimental.pallas import tpu as pltpu
from jax.sharding import Mesh
from jax.sharding import PartitionSpec as P

AXES = ("z", "c", "x", "y")
SIZES = (8, 2, 4, 4)
BF = jnp.bfloat16
F32 = jnp.float32
VMEM_LIMIT = 44 * 1024 * 1024
GROUP = 4


def rank(q):
    out = 0
    for v, s in zip(q, SIZES):
        out = out * s + v
    return out


def pairs(move):
    z, c, x, y = SIZES
    every = [(i, j, k, l) for i in range(z) for j in range(c) for k in range(x) for l in range(y)]
    return [(rank(q), rank(move(q))) for q in every]


def z_move():
    return pairs(lambda q: ((q[0] + 1 - 2 * q[1]) % 8, q[1], q[2], q[3]))


def core_move():
    return pairs(lambda q: (q[0], 1 - q[1], q[2], q[3]))


def plane_move(stage, d):
    def move(q):
        z, c, x, y = q
        if (c == 0) == (stage == 0):
            return (z, c, (x + d) % 4, y)
        return (z, c, x, (y + d) % 4)

    return pairs(move)


def send(v, perm):
    return lax.ppermute(v, AXES, perm)


def add(*parts):
    total = parts[0].astype(F32)
    for p in parts[1:]:
        total = total + p.astype(F32)
    return total


def join(segments, *arrays, after=()):
    width = arrays[0].shape[1]

    def total(refs, terms, rows):
        picked = []
        for i, at in terms:
            if isinstance(i, tuple):
                picked.append(total(refs, (i, at), rows))
            else:
                picked.append(refs[i][at : at + rows, :])
        return picked[0] if len(picked) == 1 else add(*picked)

    def kernel(*refs):
        out = refs[-1]
        base = 0
        for rows, terms in segments:
            out[base : base + rows, :] = total(refs, terms, rows).astype(BF)
            base += rows

    rows = sum(r for r, _ in segments)
    return pl.pallas_call(
        kernel,
        out_shape=jax.ShapeDtypeStruct((rows, width), BF),
        in_specs=[pl.BlockSpec(memory_space=pltpu.VMEM)] * len(arrays)
        + [pl.BlockSpec(memory_space=pl.ANY)] * len(after),
        out_specs=pl.BlockSpec(memory_space=pltpu.VMEM),
        compiler_params=pltpu.CompilerParams(vmem_limit_bytes=16 * 1024 * 1024),
        cost_estimate=pl.CostEstimate(flops=rows, bytes_accessed=rows, transcendentals=0),
        name="join",
    )(*arrays, *after)


def tile_kernel(copies, cuts, n_parts, block, transpose, info, *refs):
    parts, tiles, outs = refs[:n_parts], refs[n_parts], refs[n_parts + 1 : n_parts + 1 + len(cuts)]
    panel, acc, held, part_sem, tile_sem = refs[n_parts + 1 + len(cuts) :]
    slots = held.shape[0]
    count = info[2 * slots]
    half = block // 2

    def tile_copy(k):
        return pltpu.make_async_copy(tiles.at[k], held.at[k], tile_sem.at[k])

    def begin(k, carry):
        tile_copy(k).start()
        return carry

    lax.fori_loop(0, count, begin, 0)
    started = []
    for i, (part, src, size, dst) in enumerate(copies):
        copy = pltpu.make_async_copy(
            parts[part].at[pl.ds(src, size)], panel.at[pl.ds(dst, size)], part_sem.at[i]
        )
        copy.start()
        started.append(copy)

    def clear(k, carry):
        at = pl.ds(pl.multiple_of(k * half, half), half)
        acc[at, :] = jnp.zeros((half, acc.shape[1]), F32)
        return carry

    lax.fori_loop(0, acc.shape[0] // half, clear, 0)
    for copy in started:
        copy.wait()

    def term(k):
        if transpose:
            src = pl.multiple_of(info[k] * half, half)
            low = panel[pl.ds(src, half), :]
            piece = jnp.concatenate([low, panel[pl.ds(src + panel.shape[0] // 2, half), :]], axis=0)
            dims = (((0,), (0,)), ((), ()))
        else:
            piece = panel[pl.ds(pl.multiple_of(info[k] * block, block), block), :]
            dims = (((1,), (0,)), ((), ()))
        return lax.dot_general(held[k], piece, dims, preferred_element_type=F32)

    def several(first, n):
        for i in range(n):
            tile_copy(first + i).wait()
        terms = [term(first + i) for i in range(n)]
        for i in range(n):
            at = pl.ds(pl.multiple_of(info[slots + first + i] * block, block), block)
            acc[at, :] += terms[i]

    def group(k, carry):
        several(k * GROUP, GROUP)
        return carry

    def single(k, carry):
        several(k, 1)
        return carry

    groups = count // GROUP
    lax.fori_loop(0, groups, group, 0)
    lax.fori_loop(groups * GROUP, count, single, 0)
    for out, ranges in zip(outs, cuts):
        base = 0
        for start, rows in ranges:

            def give(k, carry, out=out, base=base, start=start):
                at = pl.multiple_of(k * half, half)
                out[pl.ds(base + at, half), :] = acc[pl.ds(start + at, half), :].astype(BF)
                return carry

            lax.fori_loop(0, rows // half, give, 0)
            base += rows


def tile_terms(info, parts, copies, tiles, cuts, transpose):
    slots, block = tiles.shape[0], tiles.shape[1]
    rows = sum(c[2] for c in copies)
    width = parts[0].shape[1]

    def kernel(*refs):
        tile_kernel(copies, cuts, len(parts), block, transpose, *refs)

    return pl.pallas_call(
        kernel,
        out_shape=[jax.ShapeDtypeStruct((sum(n for _, n in r), width), BF) for r in cuts],
        in_specs=[pl.BlockSpec(memory_space=pltpu.SMEM)]
        + [pl.BlockSpec(memory_space=pl.ANY)] * (len(parts) + 1),
        out_specs=[pl.BlockSpec(memory_space=pltpu.VMEM)] * len(cuts),
        scratch_shapes=[
            pltpu.VMEM((rows, width), BF),
            pltpu.VMEM((rows, width), F32),
            pltpu.VMEM((slots, block, block), BF),
            pltpu.SemaphoreType.DMA((len(copies),)),
            pltpu.SemaphoreType.DMA((slots,)),
        ],
        compiler_params=pltpu.CompilerParams(vmem_limit_bytes=VMEM_LIMIT),
        cost_estimate=pl.CostEstimate(
            flops=2 * slots * block * block * width,
            bytes_accessed=2 * slots * block * block + 4 * rows * width,
            transcendentals=0,
        ),
        name="tiles_t" if transpose else "tiles",
    )(info, *parts, tiles)


def node_kernel(s0, s1, s2, s3, s4, features, weight, cotangent, output, adjoint, m0, m1):
    rows = features.shape[0]
    half = rows // 2
    term = jnp.zeros(weight.shape, F32)
    for i, message in enumerate((m0, m1)):
        at = pl.ds(i * half, half)
        summed = add(s0[at, :], s1[at, :], s2[at, :]) + add(s3[at, :], s4[at, :])
        agg = (summed + features[at, :].astype(F32)).astype(BF)
        pre = jnp.dot(agg, weight[...], preferred_element_type=F32)
        sig = jax.nn.sigmoid(pre)
        output[at, :] = (pre * sig).astype(BF)
        slope = (cotangent[at, :].astype(F32) * sig * (1.0 + pre * (1.0 - sig))).astype(BF)
        back = lax.dot_general(
            slope, weight[...], (((1,), (1,)), ((), ())), preferred_element_type=F32
        ).astype(BF)
        adjoint[at, :] = back
        message[pl.ds(0, half), :] = back
        term = term + lax.dot_general(
            agg, slope, (((0,), (0,)), ((), ())), preferred_element_type=F32
        )
    wh = weight.shape[0] // 2
    m0[pl.ds(half, wh), :] = term[:wh].astype(BF)
    m1[pl.ds(half, wh), :] = term[wh:].astype(BF)


def node_step(sums, features, weight, cotangent):
    rows, width = features.shape
    message = jax.ShapeDtypeStruct(((rows + weight.shape[0]) // 2, width), BF)
    whole = jax.ShapeDtypeStruct((rows, width), BF)
    return pl.pallas_call(
        node_kernel,
        out_shape=[whole, whole, message, message],
        compiler_params=pltpu.CompilerParams(vmem_limit_bytes=16 * 1024 * 1024),
        cost_estimate=pl.CostEstimate(
            flops=6 * rows * width * width, bytes_accessed=20 * rows * width, transcendentals=rows * width
        ),
        name="nodes",
    )(*sums, features, weight, cotangent)


def row_place(cols, z, c, sign):
    return 2 * (((cols // 2 - z) * sign) % 8) + jnp.where(cols % 2 == c, 0, 1)


def gather_row(block):
    n = block.shape[0]
    other = send(block, core_move())
    own = join([(n, [(0, 0)])], block)
    parts = {0: own, 1: other}
    a, b = block, other
    for k in (1, 2, 3, 4):
        a = send(a, z_move())
        parts[2 * k] = a
        parts[2 * (8 - k) + 1] = send(a, core_move())
        if k < 4:
            b = send(join([(n, [(0, 0)])], b, after=[own]) if k == 2 else b, z_move())
            parts[2 * k + 1] = b
            parts[2 * (8 - k)] = send(b, core_move())
    return [parts[i] for i in range(16)], [(i, 0, n, i * n) for i in range(16)]


def row_cuts(n):
    order = ((0,), (1,), (8,), (9,), (6,), (7,), (4,), (5,), (2,), (3,), (11, 10), (13, 12), (15, 14))
    return [[(i * n, n) for i in blocks] for blocks in order]


def scatter_row(outs, term, weight_term):
    own, other, a4, b4, a3, b3, a2, b2, a1, b1, give_3, give_2, give_1 = outs
    n = own.shape[0]
    wh = weight_term.shape[0] // 2
    got = [send(v, core_move()) for v in (give_3, give_2, give_1)]
    a = send(join([(n, [(0, 0)]), (wh, [(1, 0)])], a4, weight_term), z_move())
    b = send(join([(n, [(0, 0)]), (wh, [(1, wh)])], b4, weight_term), z_move())
    held_a, held_b = [a], [b]
    for near_a, near_b, extra in ((a3, b3, got[0]), (a2, b2, got[1]), (a1, b1, got[2])):
        sent_b = join([(n, [(0, 0), (1, n), (2, 0)]), (wh, [(2, n)])], near_b, extra, b)
        terms = [(n, [(0, 0), (1, 0), (2, 0)]), (wh, [(2, n)])]
        sent_a = join(terms, near_a, extra, a, after=[sent_b])
        b, a = send(sent_b, z_move()), send(sent_a, z_move())
        held_a.append(a)
        held_b.append(b)
    back = send(join([(n, [(0, 0), (1, 0)])], other, b), core_move())
    rows = [(wh, [(i, n)]) for i in range(6)]
    far = send(join(rows, *held_a[:3], *held_b[:3], after=[sent_a]), core_move())
    return last_step(own, a, term, back, weight_term, far, held_a, held_b)


def last_step(own, a, term, back, weight_term, far, held_a, held_b):
    n, width = own.shape
    wh = weight_term.shape[0] // 2
    scale = 1.0 / math.sqrt(n * 256)

    def kernel(*refs):
        own, a, term, back, w, far, *held = refs[:-2]
        grad, weight = refs[-2:]
        grad[...] = (
            (add(own[...]) + add(a[:n, :])) + (add(term[...]) + add(back[...]))
        ).astype(BF)
        for h in (0, 1):
            m = [r[n:, :] for r in held[4 * h : 4 * h + 4]]
            s = [far[(3 * h + k) * wh : (3 * h + k + 1) * wh, :] for k in range(3)]
            even = add(w[h * wh : (h + 1) * wh, :], m[3]) + add(m[1], s[1])
            odd = add(s[0], m[2]) + add(s[2], m[0])
            weight[h * wh : (h + 1) * wh, :] = (even + odd) * scale

    return pl.pallas_call(
        kernel,
        out_shape=[
            jax.ShapeDtypeStruct((n, width), BF),
            jax.ShapeDtypeStruct((2 * wh, width), F32),
        ],
        compiler_params=pltpu.CompilerParams(vmem_limit_bytes=16 * 1024 * 1024),
        cost_estimate=pl.CostEstimate(flops=n, bytes_accessed=n, transcendentals=0),
        name="last",
    )(own, a, term, back, weight_term, far, *held_a, *held_b)


def scatter_plane(outs):
    a0, b0, c0, a1, b1, c1, a3, b3, c3, ab_up, ab_down, c_up, c_down = outs
    n = a0.shape[0]
    h = n // 2
    up, down = plane_move(0, 1), plane_move(0, -1)
    p, m = send(ab_up, up), send(ab_down, down)
    pa = send(join([(h, [(0, 0), (1, 0)]), (h, [(0, h)]), (h, [(2, 0)])], a1, p, c_up), up)
    ma = send(join([(h, [(0, 0)]), (h, [(0, h), (1, 0)]), (h, [(2, 0)])], a3, m, c_down), down)
    pb = send(join([(n, [(0, 0), (1, h)]), (n, [(0, n)])], b1, p), up)
    mb = send(join([(n, [(0, 0)]), (n, [(0, n), (1, h)])], b3, m), down)
    far_up = send(join([(h, [(i, 0) for i in range(3)])], a0, pa, ma), plane_move(1, 1))
    far_down = send(join([(h, [(i, h) for i in range(3)])], a0, pa, ma), plane_move(1, -1))
    pc = send(join([(h, [(0, 0), (1, n)]), (h, [(0, h)])], c1, pa), up)
    mc = send(join([(h, [(0, 0)]), (h, [(0, h), (1, n)])], c3, ma), down)
    near, far = [(i, 0) for i in range(4)], [(i, h) for i in range(3)]
    right = join([(h, near), (h, far)], b0, pb, mb, far_up)
    near, far = [(i, n) for i in range(3)], [(i, n + h) for i in range(3)] + [(3, 0)]
    left = join([(h, near), (h, far)], b0, pb, mb, far_down)
    return [c0, pc, mc, send(right, plane_move(1, 1)), send(left, plane_move(1, -1))]


def plane_cuts(n):
    cuts = []
    for da in (0, 1, 3):
        cuts += [[(4 * da * n, n)], [((4 * da + 1) * n, 2 * n)], [((4 * da + 3) * n, n)]]
    h = n // 2
    cuts += [[(8 * n, h), (9 * n, n)], [(8 * n + h, h), (10 * n, n)]]
    return cuts + [[(11 * n, h)], [(11 * n + h, h)]]


def gather_plane(adjoint, messages):
    n = adjoint.shape[0]
    h = n // 2
    wh = messages[0].shape[0] - h
    parts, copies = [], []

    def ring(v, stage):
        m = v.shape[0] // 2
        up, down = plane_move(stage, 1), plane_move(stage, -1)
        r, l = send(v, up), send(v, down)
        return l, r, send(r[:m], up), send(l[m:], down)

    for i, v in enumerate(messages):
        l, r, f_u, f_d = ring(v, 1)
        g = f_u.shape[0]
        sums = [((0, h), (4, h - g)), ((2, h), (1, h))]
        whole = join(
            [(h, [(0, 0)]), (h, [(1, 0)]), (h, [(2, 0)]), (g, [(3, 0)]), (h - g, [(4, 0)]), (wh, sums)],
            v, l, r, f_u, f_d,
        )
        q_l, q_r, q_u, q_d = ring(whole, 0)
        m = q_u.shape[0]
        places = ((0, 4 * h, 0), (1, 4 * h, 4 * h), (2, 4 * h, 12 * h), (3, m, 8 * h), (4, 4 * h - m, 8 * h + m))
        copies += [(len(parts) + j, 0, size, 16 * h * i + to) for j, size, to in places]
        parts += [whole, q_l, q_r, q_u, q_d]
    k, at = 4 * h, 4 * h - m
    return parts, copies, join(
        [(wh, [((i, k), (i + 3, at)), ((i + 1, k), (i + 2, k))]) for i in (0, 4)],
        *[parts[i] for i in (0, 1, 2, 4, 5, 6, 7, 9)],
    )


def local(tile_values, tile_rows, tile_cols, tile_counts, features, weight, cotangent):
    tiles = tile_values[0, 0]
    rows, cols, count = tile_rows[0, 0], tile_cols[0, 0], tile_counts[0]
    n, width = features.shape
    z, c, x, y = (lax.axis_index(a) for a in AXES)
    sign = 1 - 2 * c
    dx, dy = (rows // 4 - x) % 4, (rows % 4 - y) % 4
    da, db = jnp.where(c == 0, dx, dy), jnp.where(c == 0, dy, dx)
    db_place = jnp.where(db % 2 == 0, jnp.where(db == 0, 3, 0), jnp.where(db == 1, 1, 2))
    fwd = jnp.concatenate([row_place(cols, z, c, -sign), da * 4 + db_place, count])
    bwd = jnp.concatenate([da * 4 + (db ^ (db >> 1)), row_place(cols, z, c, sign), count])

    parts, copies = gather_row(features)
    sums = scatter_plane(tile_terms(fwd, parts, copies, tiles, plane_cuts(n), False))
    output, adjoint, *messages = node_step(sums, features, weight, cotangent)
    parts, copies, w = gather_plane(adjoint, messages)
    w = join([(w.shape[0], [(0, 0), (1, 0)])], w, send(w, core_move()))
    outs = tile_terms(bwd, parts, copies, tiles, row_cuts(n), True)
    grad, w = scatter_row(outs, adjoint, w)
    return (output, grad, w)


def solution(mesh):
    grid = Mesh(mesh.devices.reshape(SIZES), AXES)
    row, rep = ("z", "c"), ("x", "y")
    placed = (
        P(row, rep, None, None, None),
        P(row, rep, None),
        P(row, rep, None),
        P(row, rep),
        P(AXES, None),
        P(),
        P(AXES, None),
    )
    return jax.shard_map(
        local,
        mesh=grid,
        in_specs=placed,
        out_specs=(P(AXES, None), P(AXES, None), P()),
        check_vma=False,
    )
```

```python
import math

import jax
import jax.numpy as jnp
from jax import lax
from jax.experimental import pallas as pl
from jax.experimental.pallas import tpu as pltpu
from jax.sharding import Mesh
from jax.sharding import PartitionSpec as P

AXES = ("z", "c", "x", "y")
SIZES = (8, 2, 4, 4)
BF = jnp.bfloat16
F32 = jnp.float32
VMEM_LIMIT = 44 * 1024 * 1024
GROUP = 4


def rank(q):
    out = 0
    for v, s in zip(q, SIZES):
        out = out * s + v
    return out


def pairs(move):
    z, c, x, y = SIZES
    every = [(i, j, k, l) for i in range(z) for j in range(c) for k in range(x) for l in range(y)]
    return [(rank(q), rank(move(q))) for q in every]


def z_move():
    return pairs(lambda q: ((q[0] + 1 - 2 * q[1]) % 8, q[1], q[2], q[3]))


def core_move():
    return pairs(lambda q: (q[0], 1 - q[1], q[2], q[3]))


def plane_move(stage, d):
    def move(q):
        z, c, x, y = q
        if (c == 0) == (stage == 0):
            return (z, c, (x + d) % 4, y)
        return (z, c, x, (y + d) % 4)

    return pairs(move)


def send(v, perm):
    return lax.ppermute(v, AXES, perm)


def add(*parts):
    total = parts[0].astype(F32)
    for p in parts[1:]:
        total = total + p.astype(F32)
    return total


def join(segments, *arrays, after=()):
    width = arrays[0].shape[1]

    def total(refs, terms, rows):
        picked = []
        for i, at in terms:
            if isinstance(i, tuple):
                picked.append(total(refs, (i, at), rows))
            else:
                picked.append(refs[i][at : at + rows, :])
        return picked[0] if len(picked) == 1 else add(*picked)

    def kernel(*refs):
        out = refs[-1]
        base = 0
        for rows, terms in segments:
            out[base : base + rows, :] = total(refs, terms, rows).astype(BF)
            base += rows

    rows = sum(r for r, _ in segments)
    return pl.pallas_call(
        kernel,
        out_shape=jax.ShapeDtypeStruct((rows, width), BF),
        in_specs=[pl.BlockSpec(memory_space=pltpu.VMEM)] * len(arrays)
        + [pl.BlockSpec(memory_space=pl.ANY)] * len(after),
        out_specs=pl.BlockSpec(memory_space=pltpu.VMEM),
        compiler_params=pltpu.CompilerParams(vmem_limit_bytes=16 * 1024 * 1024),
        cost_estimate=pl.CostEstimate(flops=rows, bytes_accessed=rows, transcendentals=0),
        name="join",
    )(*arrays, *after)


def tile_kernel(copies, cuts, n_parts, block, transpose, info, *refs):
    parts, tiles, outs = refs[:n_parts], refs[n_parts], refs[n_parts + 1 : n_parts + 1 + len(cuts)]
    panel, acc, held, part_sem, tile_sem = refs[n_parts + 1 + len(cuts) :]
    slots = held.shape[0]
    count = info[2 * slots]
    half = block // 2

    def tile_copy(k):
        return pltpu.make_async_copy(tiles.at[k], held.at[k], tile_sem.at[k])

    def begin(k, carry):
        tile_copy(k).start()
        return carry

    lax.fori_loop(0, count, begin, 0)
    started = []
    for i, (part, src, size, dst) in enumerate(copies):
        copy = pltpu.make_async_copy(
            parts[part].at[pl.ds(src, size)], panel.at[pl.ds(dst, size)], part_sem.at[i]
        )
        copy.start()
        started.append(copy)

    def clear(k, carry):
        at = pl.ds(pl.multiple_of(k * half, half), half)
        acc[at, :] = jnp.zeros((half, acc.shape[1]), F32)
        return carry

    lax.fori_loop(0, acc.shape[0] // half, clear, 0)
    for copy in started:
        copy.wait()

    def term(k):
        if transpose:
            src = pl.multiple_of(info[k] * half, half)
            low = panel[pl.ds(src, half), :]
            piece = jnp.concatenate([low, panel[pl.ds(src + panel.shape[0] // 2, half), :]], axis=0)
            dims = (((0,), (0,)), ((), ()))
        else:
            piece = panel[pl.ds(pl.multiple_of(info[k] * block, block), block), :]
            dims = (((1,), (0,)), ((), ()))
        return lax.dot_general(held[k], piece, dims, preferred_element_type=F32)

    def several(first, n):
        for i in range(n):
            tile_copy(first + i).wait()
        terms = [term(first + i) for i in range(n)]
        for i in range(n):
            at = pl.ds(pl.multiple_of(info[slots + first + i] * block, block), block)
            acc[at, :] += terms[i]

    def group(k, carry):
        several(k * GROUP, GROUP)
        return carry

    def single(k, carry):
        several(k, 1)
        return carry

    groups = count // GROUP
    lax.fori_loop(0, groups, group, 0)
    lax.fori_loop(groups * GROUP, count, single, 0)
    for out, ranges in zip(outs, cuts):
        base = 0
        for start, rows in ranges:

            def give(k, carry, out=out, base=base, start=start):
                at = pl.multiple_of(k * half, half)
                out[pl.ds(base + at, half), :] = acc[pl.ds(start + at, half), :].astype(BF)
                return carry

            lax.fori_loop(0, rows // half, give, 0)
            base += rows


def tile_terms(info, parts, copies, tiles, cuts, transpose):
    slots, block = tiles.shape[0], tiles.shape[1]
    rows = sum(c[2] for c in copies)
    width = parts[0].shape[1]

    def kernel(*refs):
        tile_kernel(copies, cuts, len(parts), block, transpose, *refs)

    return pl.pallas_call(
        kernel,
        out_shape=[jax.ShapeDtypeStruct((sum(n for _, n in r), width), BF) for r in cuts],
        in_specs=[pl.BlockSpec(memory_space=pltpu.SMEM)]
        + [pl.BlockSpec(memory_space=pl.ANY)] * (len(parts) + 1),
        out_specs=[pl.BlockSpec(memory_space=pltpu.VMEM)] * len(cuts),
        scratch_shapes=[
            pltpu.VMEM((rows, width), BF),
            pltpu.VMEM((rows, width), F32),
            pltpu.VMEM((slots, block, block), BF),
            pltpu.SemaphoreType.DMA((len(copies),)),
            pltpu.SemaphoreType.DMA((slots,)),
        ],
        compiler_params=pltpu.CompilerParams(vmem_limit_bytes=VMEM_LIMIT),
        cost_estimate=pl.CostEstimate(
            flops=2 * slots * block * block * width,
            bytes_accessed=2 * slots * block * block + 4 * rows * width,
            transcendentals=0,
        ),
        name="tiles_t" if transpose else "tiles",
    )(info, *parts, tiles)


def node_kernel(s0, s1, s2, s3, s4, features, weight, cotangent, output, adjoint, m0, m1):
    rows = features.shape[0]
    half = rows // 2
    term = jnp.zeros(weight.shape, F32)
    for i, message in enumerate((m0, m1)):
        at = pl.ds(i * half, half)
        summed = add(s0[at, :], s1[at, :], s2[at, :]) + add(s3[at, :], s4[at, :])
        agg = (summed + features[at, :].astype(F32)).astype(BF)
        pre = jnp.dot(agg, weight[...], preferred_element_type=F32)
        sig = jax.nn.sigmoid(pre)
        output[at, :] = (pre * sig).astype(BF)
        slope = (cotangent[at, :].astype(F32) * sig * (1.0 + pre * (1.0 - sig))).astype(BF)
        back = lax.dot_general(
            slope, weight[...], (((1,), (1,)), ((), ())), preferred_element_type=F32
        ).astype(BF)
        adjoint[at, :] = back
        message[pl.ds(0, half), :] = back
        term = term + lax.dot_general(
            agg, slope, (((0,), (0,)), ((), ())), preferred_element_type=F32
        )
    wh = weight.shape[0] // 2
    m0[pl.ds(half, wh), :] = term[:wh].astype(BF)
    m1[pl.ds(half, wh), :] = term[wh:].astype(BF)


def node_step(sums, features, weight, cotangent):
    rows, width = features.shape
    message = jax.ShapeDtypeStruct(((rows + weight.shape[0]) // 2, width), BF)
    whole = jax.ShapeDtypeStruct((rows, width), BF)
    return pl.pallas_call(
        node_kernel,
        out_shape=[whole, whole, message, message],
        compiler_params=pltpu.CompilerParams(vmem_limit_bytes=16 * 1024 * 1024),
        cost_estimate=pl.CostEstimate(
            flops=6 * rows * width * width, bytes_accessed=20 * rows * width, transcendentals=rows * width
        ),
        name="nodes",
    )(*sums, features, weight, cotangent)


def row_place(cols, z, c, sign):
    return 2 * (((cols // 2 - z) * sign) % 8) + jnp.where(cols % 2 == c, 0, 1)


def gather_row(block):
    n = block.shape[0]
    other = send(block, core_move())
    own = join([(n, [(0, 0)])], block)
    parts = {0: own, 1: other}
    a, b = block, other
    for k in (1, 2, 3, 4):
        a = send(a, z_move())
        parts[2 * k] = a
        parts[2 * (8 - k) + 1] = send(a, core_move())
        if k < 4:
            b = send(join([(n, [(0, 0)])], b, after=[own]) if k == 2 else b, z_move())
            parts[2 * k + 1] = b
            parts[2 * (8 - k)] = send(b, core_move())
    return [parts[i] for i in range(16)], [(i, 0, n, i * n) for i in range(16)]


def row_cuts(n):
    order = ((0,), (1,), (8,), (9,), (6,), (7,), (4,), (5,), (2,), (3,), (11, 10, 13, 12, 15, 14))
    return [[(i * n, n) for i in blocks] for blocks in order]


def scatter_row(outs, term, weight_term):
    own, other, a4, b4, a3, b3, a2, b2, a1, b1, give = outs
    n = own.shape[0]
    wh = weight_term.shape[0] // 2
    got = send(give, core_move())
    a = send(join([(n, [(0, 0)]), (wh, [(1, 0)])], a4, weight_term), z_move())
    b = send(join([(n, [(0, 0)]), (wh, [(1, wh)])], b4, weight_term), z_move())
    held_a, held_b = [a], [b]
    for near_a, near_b, at in ((a3, b3, 0), (a2, b2, 2 * n), (a1, b1, 4 * n)):
        sent_b = join([(n, [(0, 0), (1, at + n), (2, 0)]), (wh, [(2, n)])], near_b, got, b)
        terms = [(n, [(0, 0), (1, at), (2, 0)]), (wh, [(2, n)])]
        sent_a = join(terms, near_a, got, a, after=[sent_b])
        b, a = send(sent_b, z_move()), send(sent_a, z_move())
        held_a.append(a)
        held_b.append(b)
    back = send(join([(n, [(0, 0), (1, 0)])], other, b), core_move())
    rows = [(wh, [(i, n)]) for i in range(6)]
    far = send(join(rows, *held_a[:3], *held_b[:3], after=[sent_a]), core_move())
    return last_step(own, a, term, back, weight_term, far, held_a, held_b)


def last_step(own, a, term, back, weight_term, far, held_a, held_b):
    n, width = own.shape
    wh = weight_term.shape[0] // 2
    scale = 1.0 / math.sqrt(n * 256)

    def kernel(*refs):
        own, a, term, back, w, far, *held = refs[:-2]
        grad, weight = refs[-2:]
        grad[...] = (
            (add(own[...]) + add(a[:n, :])) + (add(term[...]) + add(back[...]))
        ).astype(BF)
        for h in (0, 1):
            m = [r[n:, :] for r in held[4 * h : 4 * h + 4]]
            s = [far[(3 * h + k) * wh : (3 * h + k + 1) * wh, :] for k in range(3)]
            even = add(w[h * wh : (h + 1) * wh, :], m[3]) + add(m[1], s[1])
            odd = add(s[0], m[2]) + add(s[2], m[0])
            weight[h * wh : (h + 1) * wh, :] = (even + odd) * scale

    return pl.pallas_call(
        kernel,
        out_shape=[
            jax.ShapeDtypeStruct((n, width), BF),
            jax.ShapeDtypeStruct((2 * wh, width), F32),
        ],
        compiler_params=pltpu.CompilerParams(vmem_limit_bytes=16 * 1024 * 1024),
        cost_estimate=pl.CostEstimate(flops=n, bytes_accessed=n, transcendentals=0),
        name="last",
    )(own, a, term, back, weight_term, far, *held_a, *held_b)


def scatter_plane(outs):
    a0, b0, c0, a1, b1, c1, a3, b3, c3, ab_up, ab_down, c_up, c_down = outs
    n = a0.shape[0]
    h = n // 2
    up, down = plane_move(0, 1), plane_move(0, -1)
    p, m = send(ab_up, up), send(ab_down, down)
    pa = send(join([(h, [(0, 0), (1, 0)]), (h, [(0, h)]), (h, [(2, 0)])], a1, p, c_up), up)
    ma = send(join([(h, [(0, 0)]), (h, [(0, h), (1, 0)]), (h, [(2, 0)])], a3, m, c_down), down)
    pb = send(join([(n, [(0, 0), (1, h)]), (n, [(0, n)])], b1, p), up)
    mb = send(join([(n, [(0, 0)]), (n, [(0, n), (1, h)])], b3, m), down)
    far_up = send(join([(h, [(i, 0) for i in range(3)])], a0, pa, ma), plane_move(1, 1))
    far_down = send(join([(h, [(i, h) for i in range(3)])], a0, pa, ma), plane_move(1, -1))
    pc = send(join([(h, [(0, 0), (1, n)]), (h, [(0, h)])], c1, pa), up)
    mc = send(join([(h, [(0, 0)]), (h, [(0, h), (1, n)])], c3, ma), down)
    near, far = [(i, 0) for i in range(4)], [(i, h) for i in range(3)]
    right = join([(h, near), (h, far)], b0, pb, mb, far_up)
    near, far = [(i, n) for i in range(3)], [(i, n + h) for i in range(3)] + [(3, 0)]
    left = join([(h, near), (h, far)], b0, pb, mb, far_down)
    return [c0, pc, mc, send(right, plane_move(1, 1)), send(left, plane_move(1, -1))]


def plane_cuts(n):
    cuts = []
    for da in (0, 1, 3):
        cuts += [[(4 * da * n, n)], [((4 * da + 1) * n, 2 * n)], [((4 * da + 3) * n, n)]]
    h = n // 2
    cuts += [[(8 * n, h), (9 * n, n)], [(8 * n + h, h), (10 * n, n)]]
    return cuts + [[(11 * n, h)], [(11 * n + h, h)]]


def gather_plane(adjoint, messages):
    n = adjoint.shape[0]
    h = n // 2
    wh = messages[0].shape[0] - h
    parts, copies = [], []

    def ring(v, stage):
        m = v.shape[0] // 2
        up, down = plane_move(stage, 1), plane_move(stage, -1)
        r, l = send(v, up), send(v, down)
        return l, r, send(r[:m], up), send(l[m:], down)

    for i, v in enumerate(messages):
        l, r, f_u, f_d = ring(v, 1)
        g = f_u.shape[0]
        sums = [((0, h), (4, h - g)), ((2, h), (1, h))]
        whole = join(
            [(h, [(0, 0)]), (h, [(1, 0)]), (h, [(2, 0)]), (g, [(3, 0)]), (h - g, [(4, 0)]), (wh, sums)],
            v, l, r, f_u, f_d,
        )
        q_l, q_r, q_u, q_d = ring(whole, 0)
        m = q_u.shape[0]
        places = ((0, 4 * h, 0), (1, 4 * h, 4 * h), (2, 4 * h, 12 * h), (3, m, 8 * h), (4, 4 * h - m, 8 * h + m))
        copies += [(len(parts) + j, 0, size, 16 * h * i + to) for j, size, to in places]
        parts += [whole, q_l, q_r, q_u, q_d]
    k, at = 4 * h, 4 * h - m
    return parts, copies, join(
        [(wh, [((i, k), (i + 3, at)), ((i + 1, k), (i + 2, k))]) for i in (0, 4)],
        *[parts[i] for i in (0, 1, 2, 4, 5, 6, 7, 9)],
    )


def local(tile_values, tile_rows, tile_cols, tile_counts, features, weight, cotangent):
    tiles = tile_values[0, 0]
    rows, cols, count = tile_rows[0, 0], tile_cols[0, 0], tile_counts[0]
    n, width = features.shape
    z, c, x, y = (lax.axis_index(a) for a in AXES)
    sign = 1 - 2 * c
    dx, dy = (rows // 4 - x) % 4, (rows % 4 - y) % 4
    da, db = jnp.where(c == 0, dx, dy), jnp.where(c == 0, dy, dx)
    db_place = jnp.where(db % 2 == 0, jnp.where(db == 0, 3, 0), jnp.where(db == 1, 1, 2))
    fwd = jnp.concatenate([row_place(cols, z, c, -sign), da * 4 + db_place, count])
    bwd = jnp.concatenate([da * 4 + (db ^ (db >> 1)), row_place(cols, z, c, sign), count])

    parts, copies = gather_row(features)
    sums = scatter_plane(tile_terms(fwd, parts, copies, tiles, plane_cuts(n), False))
    output, adjoint, *messages = node_step(sums, features, weight, cotangent)
    parts, copies, w = gather_plane(adjoint, messages)
    w = join([(w.shape[0], [(0, 0), (1, 0)])], w, send(w, core_move()))
    outs = tile_terms(bwd, parts, copies, tiles, row_cuts(n), True)
    grad, w = scatter_row(outs, adjoint, w)
    return (output, grad, w)


def solution(mesh):
    grid = Mesh(mesh.devices.reshape(SIZES), AXES)
    row, rep = ("z", "c"), ("x", "y")
    placed = (
        P(row, rep, None, None, None),
        P(row, rep, None),
        P(row, rep, None),
        P(row, rep),
        P(AXES, None),
        P(),
        P(AXES, None),
    )
    return jax.shard_map(
        local,
        mesh=grid,
        in_specs=placed,
        out_specs=(P(AXES, None), P(AXES, None), P()),
        check_vma=False,
    )
```
